32 devices in a mesh: ctx: 8 (over y, x, core), head: 4 (over z).
Axes of the slice: x: 2, y: 2, z: 4, core: 2. Of those that a mesh axis runs over, the one named last changes fastest.
Arguments:
- attn_query: bfloat16 [4096, 32, 128], P('ctx', 'head'), may hold values from -6 to 6
- attn_key: bfloat16 [4096, 8, 128], P('ctx', 'head'), may hold values from -6 to 6
- attention_value: bfloat16 [4096, 8, 128], P('ctx', 'head'), may hold values from -6 to 6
- delta_query: bfloat16 [4096, 32, 128], P('ctx', 'head'), may hold values from -6 to 6
- delta_key: bfloat16 [4096, 32, 128], P('ctx', 'head'), may hold values from -6 to 6
- delta_value: bfloat16 [4096, 32, 128], P('ctx', 'head'), may hold values from -6 to 6
- log_decay: float32 [32, 4096], P('head', 'ctx'), may hold values from -0.8 to 0, as said below
- beta_gate: float32 [32, 4096], P('head', 'ctx'), may hold values from 0.1 to 0.9
Outputs:
- attn_out: bfloat16 [4096, 4096], P(('ctx', 'head'))
- delta_out: bfloat16 [4096, 4096], P(('ctx', 'head'))
The draws below stay inside these ranges and needn't reach their ends.
Inputs may be any that keep to these rules, and one draw needn't show every extreme that they name: `log_decay`: each entry is the natural logarithm of a decay factor of one head at one token.
All inputs are finite; a program needn't handle non-finite values.
Results may differ from the reference program's by a relative error of at most 0.0045.
Values may be sent and summed in bfloat16 or wider, within the bound.
A program may use at most 128 MiB of HBM per device.

```python
import math
import jax
import jax.numpy as jnp
from jax import lax

HEAD_SIZE = 128
QUERY_HEADS = 32
KEY_VALUE_HEADS = 8
DELTA_HEADS = 32
WINDOW = 1024
SPAN = 64
TOK_DEV = 512
SEQUENCE_TOKENS = 4096


def draw_attn_query(key, part):
    random_key = jax.random.fold_in(key, 1)
    sampled_values = jax.random.truncated_normal(random_key, -6.0, 6.0, (SEQUENCE_TOKENS, QUERY_HEADS, HEAD_SIZE), jnp.float32)
    return sampled_values.astype(jnp.bfloat16)


def draw_attn_key(key, part):
    random_key = jax.random.fold_in(key, 2)
    sampled_values = jax.random.truncated_normal(random_key, -6.0, 6.0, (SEQUENCE_TOKENS, KEY_VALUE_HEADS, HEAD_SIZE), jnp.float32)
    return sampled_values.astype(jnp.bfloat16)


def draw_delta_key(key, part):
    sub_rank = max(2, HEAD_SIZE // 8)
    head_keys = jax.random.split(jax.random.fold_in(key, 31), DELTA_HEADS)
    orders = jax.vmap(lambda one_key: jax.random.permutation(one_key, HEAD_SIZE))(head_keys)
    inside = orders < sub_rank
    spread_level = math.sqrt(sub_rank / SEQUENCE_TOKENS)
    scale_table = jnp.where(inside, 1.0, spread_level).astype(jnp.float32)
    random_key = jax.random.fold_in(key, 32)
    sampled_values = jax.random.truncated_normal(random_key, -6.0, 6.0, (SEQUENCE_TOKENS, DELTA_HEADS, HEAD_SIZE), jnp.float32)
    sampled_values = sampled_values * scale_table[None, :, :]
    return sampled_values.astype(jnp.bfloat16)


def draw_log_decay(key, part):
    fast_count = DELTA_HEADS // 2
    rank_order = jax.random.permutation(jax.random.fold_in(key, 21), DELTA_HEADS)
    quick_head = rank_order < fast_count
    fast_rate = jnp.exp(jax.random.uniform(jax.random.fold_in(key, 22), (DELTA_HEADS,), jnp.float32, math.log(1.0 / 50.0), math.log(1.0 / 30.0)))
    slow_rate = jnp.exp(jax.random.uniform(jax.random.fold_in(key, 23), (DELTA_HEADS,), jnp.float32, math.log(0.05), math.log(0.5))) / SEQUENCE_TOKENS
    decay_speed = jnp.where(quick_head, fast_rate, slow_rate)
    multiplier = jnp.exp(jax.random.uniform(jax.random.fold_in(key, 24), (DELTA_HEADS, SEQUENCE_TOKENS // TOK_DEV), jnp.float32, math.log(0.6), math.log(1.7)))
    multiplier = jnp.repeat(multiplier, TOK_DEV, axis=1)
    third_length = SEQUENCE_TOKENS // 3
    spike_position = jnp.arange(3)[None, :] * third_length + jax.random.randint(jax.random.fold_in(key, 25), (DELTA_HEADS, 3), 0, third_length)
    spike_drop = jnp.log(jax.random.uniform(jax.random.fold_in(key, 26), (DELTA_HEADS, 3), jnp.float32, 0.5, 0.8))
    token_position = jnp.arange(SEQUENCE_TOKENS)
    spike_sum = jnp.sum(jnp.where(token_position[None, None, :] == spike_position[:, :, None], spike_drop[:, :, None], 0.0), axis=1)
    sampled_values = jnp.where(quick_head[:, None], 0.0, spike_sum) - decay_speed[:, None] * multiplier
    return sampled_values.astype(jnp.float32)


def block_levels(own_key, extent, cuts, smallest, largest):
    def one(position, blocks):
        heights = jax.random.uniform(jax.random.fold_in(jax.random.fold_in(own_key, 6), position), (blocks,), jnp.float32, smallest / len(cuts), largest / len(cuts))
        return jnp.repeat(jnp.exp(heights), extent[position] // blocks).reshape((-1,) + (1,) * (len(extent) - position - 1))

    level = one(*cuts[0])
    for cut in cuts[1:]:
        level = level * one(*cut)
    return level


def noise(rng, extent, deviation, reach, pieces=(), held_as=jnp.bfloat16):
    level = block_levels(rng, extent, pieces, -0.22, 0.18) if pieces else 1.0
    array = jax.random.normal(rng, extent, jnp.float32) * deviation * level
    return jnp.minimum(jnp.maximum(array, -reach), reach).astype(held_as)


def setup_inputs(seed: int = 0) -> dict:
    key_list = jax.random.split(jax.random.key(seed), 9)
    return {
        "attn_query": draw_attn_query(jax.random.fold_in(key_list[8], 71), 0),
        "attn_key": draw_attn_key(jax.random.fold_in(key_list[8], 71), 0),
        "attention_value": noise(key_list[2], (SEQUENCE_TOKENS, KEY_VALUE_HEADS, HEAD_SIZE), 1.0, 6.0, ((0, 8), (1, 4))),
        "delta_query": noise(key_list[3], (SEQUENCE_TOKENS, DELTA_HEADS, HEAD_SIZE), 1.0, 6.0, ((0, 8), (1, 4))),
        "delta_key": draw_delta_key(jax.random.fold_in(key_list[8], 71), 0),
        "delta_value": noise(key_list[5], (SEQUENCE_TOKENS, DELTA_HEADS, HEAD_SIZE), 1.0, 6.0, ((0, 8), (1, 4))),
        "log_decay": draw_log_decay(jax.random.fold_in(key_list[8], 71), 0),
        "beta_gate": jnp.clip(0.1 + 0.79999997 * jax.random.uniform(key_list[7], (DELTA_HEADS, SEQUENCE_TOKENS), jnp.float32) ** block_levels(key_list[7], (DELTA_HEADS, SEQUENCE_TOKENS), ((0, 4), (1, 8)), -0.2, 0.2), 0.1, 0.9),
    }


norm_epsilon = 1e-06

def product(form, left, right):
    return jnp.einsum(form, left, right, precision=lax.Precision.HIGHEST)

def normalize(tensor, scale_factor):
    widened = tensor.astype(jnp.float32)
    return widened / jnp.sqrt(lax.optimization_barrier(jnp.sum(widened * widened, axis=-1, keepdims=True)) + norm_epsilon) * scale_factor

def invert_unit(strict):
    span_len = strict.shape[-1]
    identity = jnp.eye(span_len, dtype=strict.dtype)
    inverse = identity - strict
    power_term = strict
    for level in range(1, max(1, (span_len - 1).bit_length())):
        power_term = product('hij,hjk->hik', power_term, power_term)
        inverse = inverse + product('hij,hjk->hik', inverse, power_term)
    return inverse

def prepare(query_unit, key_unit, beta_rows, log_rows):
    span_len = log_rows.shape[1]
    cumulative = jnp.cumsum(log_rows, axis=1)
    row_index = jnp.arange(span_len, dtype=jnp.int32)[:, None]
    col_index = jnp.arange(span_len, dtype=jnp.int32)[None, :]
    log_gap = cumulative[:, :, None] - cumulative[:, None, :]
    decay_ratio = jnp.exp(jnp.where(row_index >= col_index, log_gap, -jnp.inf))
    key_inner = product('hcd,hed->hce', key_unit, key_unit)
    strict = jnp.where(row_index > col_index, beta_rows[:, :, None] * decay_ratio * key_inner, 0.0)
    causal = product('hcd,hed->hce', query_unit, key_unit) * decay_ratio
    return (cumulative, invert_unit(strict), causal)

def advance(carried, query_unit, key_unit, value_rows, beta_rows, prepared):
    cumulative, inverse, causal = prepared
    leading = jnp.exp(cumulative)
    projected = product('hcd,hvd->hcv', key_unit, carried)
    right_side = beta_rows[:, :, None] * (value_rows - leading[:, :, None] * projected)
    weighted = product('hce,hev->hcv', inverse, right_side)
    result = leading[:, :, None] * product('hcd,hvd->hcv', query_unit, carried) + product('hts,hsv->htv', causal, weighted)
    trailing = jnp.exp(cumulative[:, -1:] - cumulative)
    updated = jnp.exp(cumulative[:, -1])[:, None, None] * carried + product('hsv,hsd->hvd', trailing[:, :, None] * weighted, key_unit)
    return (updated, result)

def to_spans(tensor, span_len):
    return tensor.reshape(tensor.shape[0] // span_len, span_len, tensor.shape[1], tensor.shape[2]).transpose(0, 2, 1, 3)

def gate_spans(tensor, span_len):
    return tensor.reshape(tensor.shape[0], tensor.shape[1] // span_len, span_len).transpose(1, 0, 2)

def from_spans(tensor):
    return tensor.transpose(0, 2, 1, 3).reshape(tensor.shape[0] * tensor.shape[2], tensor.shape[1] * tensor.shape[3])

def reference(attn_query, attn_key, attention_value, delta_query, delta_key, delta_value, log_decay, beta_gate):
    block_length = math.gcd(512, SEQUENCE_TOKENS)
    group_count = QUERY_HEADS // KEY_VALUE_HEADS
    key_padded = jnp.pad(attn_key, ((WINDOW, 0), (0, 0), (0, 0)))
    value_padded = jnp.pad(attention_value, ((WINDOW, 0), (0, 0), (0, 0)))

    def attend_block(block_index):
        block_start = block_index * block_length
        query_tile_block = lax.dynamic_slice_in_dim(attn_query, block_start, block_length, 0)
        query_tile_block = query_tile_block.reshape(block_length, KEY_VALUE_HEADS, group_count, HEAD_SIZE).astype(jnp.float32)
        key_block = lax.dynamic_slice_in_dim(key_padded, block_start, WINDOW + block_length, 0).astype(jnp.float32)
        value_block = lax.dynamic_slice_in_dim(value_padded, block_start, WINDOW + block_length, 0).astype(jnp.float32)
        scores = jnp.einsum('qgrd,kgd->grqk', query_tile_block, key_block) * (1.0 / math.sqrt(HEAD_SIZE))
        query_pos = block_start + jnp.arange(block_length, dtype=jnp.int32)
        key_pos = block_start - WINDOW + jnp.arange(WINDOW + block_length, dtype=jnp.int32)
        allowed = (key_pos[None, :] <= query_pos[:, None]) & (key_pos[None, :] > query_pos[:, None] - WINDOW) & (key_pos[None, :] >= 0)
        scores = jnp.where(allowed, scores, -jnp.inf)
        row_max = lax.optimization_barrier(jnp.max(scores, axis=-1, keepdims=True))
        unnormed = jnp.exp(scores - row_max)
        row_total = lax.optimization_barrier(jnp.sum(unnormed, axis=-1))
        weights = unnormed.astype(jnp.bfloat16)
        mixed_out = jnp.einsum('grqk,kgd->qgrd', weights.astype(jnp.float32), value_block)
        mixed_out = mixed_out / jnp.transpose(row_total, (2, 0, 1))[..., None]
        return mixed_out.reshape(block_length, QUERY_HEADS * HEAD_SIZE).astype(jnp.bfloat16)
    attn_blocks = lax.map(attend_block, jnp.arange(SEQUENCE_TOKENS // block_length, dtype=jnp.int32))
    attn_out = attn_blocks.reshape(SEQUENCE_TOKENS, QUERY_HEADS * HEAD_SIZE)
    query_unit = normalize(delta_query, 1.0 / math.sqrt(HEAD_SIZE))
    key_unit = normalize(delta_key, 1.0)
    inputs = (to_spans(query_unit, SPAN), to_spans(key_unit, SPAN), to_spans(delta_value.astype(jnp.float32), SPAN), gate_spans(beta_gate, SPAN), gate_spans(log_decay, SPAN))

    def span_step(carried, span_inputs):
        query_part, key_part, value_part, beta_part, log_part = span_inputs
        prepared = prepare(query_part, key_part, beta_part, log_part)
        return advance(carried, query_part, key_part, value_part, beta_part, prepared)
    start_state = jnp.zeros((DELTA_HEADS, HEAD_SIZE, HEAD_SIZE), jnp.float32)
    final_state, span_outs = lax.scan(span_step, start_state, inputs)
    delta_out = from_spans(span_outs).astype(jnp.bfloat16)
    return (attn_out, delta_out)
```

```python
import functools
import math

import jax
import jax.numpy as jnp
from jax import lax
from jax.experimental import pallas as pl
from jax.experimental.pallas import tpu as pltpu
from jax.sharding import PartitionSpec as P

WINDOW = 1024
CHUNK = 128
PAIR = 2
norm_epsilon = 1e-06
F32, BF16 = jnp.float32, jnp.bfloat16
VMEM_BYTES = 56 * 1024 * 1024


def dot(a, b):
    return lax.dot_general(a, b, (((1,), (0,)), ((), ())), preferred_element_type=F32)


def dot_nt(a, b):
    return lax.dot_general(a, b, (((1,), (1,)), ((), ())), preferred_element_type=F32)


def split(x):
    high = x.astype(BF16)
    return high, (x - high.astype(F32)).astype(BF16)


def dot_square(a, b):
    ah, al = split(a)
    bh, bl = split(b)
    right = jnp.concatenate((bh, bl), axis=1)
    both = dot(jnp.concatenate((ah, al), axis=1), jnp.concatenate((right, right), axis=0))
    width = b.shape[1]
    return both[:, :width] + both[:, width:]


def dot_wide(a, b):
    ah, al = split(a)
    bh, bl = split(b)
    return dot(jnp.concatenate((ah, al), axis=1), jnp.concatenate((bh, bh), axis=0)) + dot(ah, bl)


def row_cumsum(row, upper):
    a = row.astype(BF16)
    rest = row - a.astype(F32)
    b = rest.astype(BF16)
    c = (rest - b.astype(F32)).astype(BF16)
    return dot(a, upper) + (dot(b, upper) + dot(c, upper))


def delta_spans(parts, head_dim):
    size = CHUNK
    row = lax.broadcasted_iota(jnp.int32, (size, size), 0)
    col = lax.broadcasted_iota(jnp.int32, (size, size), 1)
    upper = (row <= col).astype(BF16)
    eye = (row == col).astype(F32)
    state = []
    for q, k, v, log_row, beta_row in parts:
        qb, kb = q.astype(BF16), k.astype(BF16)
        rk = lax.rsqrt(jnp.sum(k * k, axis=1, keepdims=True) + norm_epsilon)
        rq = lax.rsqrt(jnp.sum(q * q, axis=1, keepdims=True) + norm_epsilon) / math.sqrt(head_dim)
        g = row_cumsum(jnp.broadcast_to(log_row, (8, size)), upper)[0:1, :]
        g_row = jnp.broadcast_to(g, (size, size))
        g_col = g_row.T
        b_col = jnp.broadcast_to(beta_row, (size, size)).T
        rk_row = jnp.broadcast_to(rk, (size, size)).T
        ratio = jnp.exp(jnp.where(row >= col, g_col - g_row, -jnp.inf)) * rk_row
        strict = jnp.where(row > col, b_col * rk * ratio * dot_nt(kb, kb), 0.0)
        causal = rq * ratio * dot_nt(qb, kb)
        state.append((strict, causal, g_col, b_col, rk, rq, g))
    inverse = []
    first = (row // 2 == col // 2) & (row > col)
    for s in state:
        inverse.append(eye - jnp.where(first, s[0], 0.0))
    block = 2
    while block < size:
        mask = (row // (2 * block) == col // (2 * block)) & (row // block > col // block)
        half = [dot_square(t, jnp.where(mask, s[0], 0.0)) for t, s in zip(inverse, state)]
        inverse = [t - dot_square(x, t) for t, x in zip(inverse, half)]
        block *= 2
    out = []
    for (q, k, v, _, _), t, (strict, causal, g_col, b_col, rk, rq, g) in zip(parts, inverse, state):
        lead = jnp.exp(g_col)
        weighted = dot_wide(t, jnp.concatenate((b_col * lead * rk * k, b_col * v), axis=1))
        mixed = dot_wide(causal, weighted)
        queries = lead * rq * q - mixed[:, :head_dim]
        last = g[:, size - 1 : size]
        trail = jnp.exp(last - g_col) * rk
        th, tl = split(jnp.concatenate((trail, trail), axis=1) * weighted)
        kt = k.T.astype(BF16)
        written = dot(jnp.concatenate((kt, kt), axis=1), jnp.concatenate((th, tl), axis=0))
        out.append((queries, mixed[:, head_dim:], jnp.exp(last), written))
    return out


def compose(spans, head_dim):
    zeros = jnp.zeros((head_dim, head_dim), F32)
    r = lax.broadcasted_iota(jnp.int32, (head_dim, head_dim), 0)
    c = lax.broadcasted_iota(jnp.int32, (head_dim, head_dim), 1)
    eye = (r == c).astype(F32)
    carried, results = None, []
    for queries, mixed, keep, written in spans:
        if carried is None:
            results.append((queries, mixed))
            carried = jnp.concatenate((keep * eye - written[:, :head_dim], written[:, head_dim:]), axis=1)
        else:
            both = dot_wide(queries, carried)
            results.append((both[:, :head_dim], both[:, head_dim:] + mixed))
            step = dot_wide(written[:, :head_dim], carried)
            carried = keep * carried - step + jnp.concatenate((zeros, written[:, head_dim:]), axis=1)
    return results, carried


def delta_kernel(heads, tokens, q_ref, k_ref, v_ref, log_ref, beta_ref, moved_ref, local_ref, pair_ref, fq, fk, fv):
    head_dim = q_ref.shape[1]

    @pl.when(pl.program_id(0) == 0)
    def _():
        fq[...] = q_ref[...].astype(F32)
        fk[...] = k_ref[...].astype(F32)
        fv[...] = v_ref[...].astype(F32)

    count = tokens // CHUNK
    parts = []
    for j in range(PAIR):
        h = pl.program_id(0) * PAIR + j
        for c in range(count):
            rows = pl.ds(c * CHUNK * heads + h, CHUNK, stride=heads)
            lanes = slice(c * CHUNK, (c + 1) * CHUNK)
            pick = lax.broadcasted_iota(jnp.int32, (heads, CHUNK), 0) == h
            gates = [
                jnp.sum(jnp.where(pick, ref[:, lanes], 0.0), axis=0, keepdims=True) for ref in (log_ref, beta_ref)
            ]
            parts.append((fq[rows, :], fk[rows, :], fv[rows, :], *gates))
    spans = delta_spans(parts, head_dim)
    for j in range(PAIR):
        results, carried = compose(spans[j * count : (j + 1) * count], head_dim)
        for c, (moved, local_part) in enumerate(results):
            moved_ref[j, c * CHUNK : (c + 1) * CHUNK, :] = moved
            local_ref[j, c * CHUNK : (c + 1) * CHUNK, :] = local_part
        pair_ref[j] = carried.astype(pair_ref.dtype)


def delta_local(q, k, v, log_decay, beta):
    tokens, heads, d = q.shape
    flat = [x.reshape(tokens * heads, d) for x in (q, k, v)]
    full = pl.BlockSpec((tokens * heads, d), lambda i: (0, 0))
    gate = pl.BlockSpec((heads, tokens), lambda i: (0, 0))
    per_head = pl.BlockSpec((PAIR, tokens, d), lambda i: (i, 0, 0))
    return pl.pallas_call(
        functools.partial(delta_kernel, heads, tokens),
        grid=(heads // PAIR,),
        in_specs=[full, full, full, gate, gate],
        out_specs=[per_head, per_head, pl.BlockSpec((PAIR, d, 2 * d), lambda i: (i, 0, 0))],
        out_shape=[
            jax.ShapeDtypeStruct((heads, tokens, d), F32),
            jax.ShapeDtypeStruct((heads, tokens, d), F32),
            jax.ShapeDtypeStruct((heads, d, 2 * d), BF16),
        ],
        scratch_shapes=[pltpu.VMEM((tokens * heads, d), F32)] * 3,
        compiler_params=pltpu.CompilerParams(vmem_limit_bytes=VMEM_BYTES),
        cost_estimate=pl.CostEstimate(flops=10_000_000_000, bytes_accessed=8_000_000, transcendentals=0),
        name="delta_local",
    )(*flat, log_decay, beta)


def prefix_kernel(pair_ref, state_ref):
    n, d = pair_ref.shape[0], pair_ref.shape[1]
    state = jnp.zeros((d, d), F32)
    for i in range(n):
        state_ref[i] = state.astype(state_ref.dtype)
        if i < n - 1:
            sh, sl = split(state)
            move = pair_ref[i, :, :d]
            both = dot(jnp.concatenate((move, move), axis=1), jnp.concatenate((sh, sl), axis=0))
            state = both + pair_ref[i, :, d:].astype(F32)


def final_kernel(moved_ref, local_ref, state_ref, out_ref):
    sh = state_ref[0]
    mh, ml = split(moved_ref[0])
    both = dot(jnp.concatenate((mh, ml), axis=1), jnp.concatenate((sh, sh), axis=0))
    out_ref[...] = (both + local_ref[0]).astype(BF16)


def delta_final(moved, local_part, states):
    heads, tokens, d = moved.shape
    per_head = pl.BlockSpec((1, tokens, d), lambda h: (h, 0, 0))
    return pl.pallas_call(
        final_kernel,
        grid=(heads,),
        in_specs=[per_head, per_head, pl.BlockSpec((1, d, d), lambda h: (h, 0, 0))],
        out_specs=pl.BlockSpec((tokens, d), lambda h: (0, h)),
        out_shape=jax.ShapeDtypeStruct((tokens, heads * d), BF16),
        compiler_params=pltpu.CompilerParams(vmem_limit_bytes=VMEM_BYTES),
        cost_estimate=pl.CostEstimate(flops=2_000_000_000, bytes_accessed=6_000_000, transcendentals=0),
        name="delta_final",
    )(moved, local_part, states)


def incoming_states(pairs):
    heads, d = pairs.shape[0], pairs.shape[1]
    n = lax.axis_size("ctx")
    if n == heads:
        mine = lax.all_to_all(pairs, "ctx", split_axis=0, concat_axis=0, tiled=True)
        states = pl.pallas_call(
            prefix_kernel,
            out_shape=jax.ShapeDtypeStruct((n, d, d), BF16),
            cost_estimate=pl.CostEstimate(flops=500_000_000, bytes_accessed=800_000, transcendentals=0),
            name="prefix",
        )(mine)
        return lax.all_to_all(states, "ctx", split_axis=0, concat_axis=0, tiled=True)
    transit, source = pairs[:, :, :d].astype(F32), pairs[:, :, d:].astype(F32)

    def relay(turn, inbound):
        leaving = jnp.einsum("hij,hjk->hik", transit, inbound, precision=lax.Precision.HIGHEST) + source
        return lax.ppermute(leaving, "ctx", [(i, i + 1) for i in range(n - 1)])

    return lax.fori_loop(0, n - 1, relay, jnp.zeros((heads, d, d), F32)).astype(BF16)


ROWS = 128


def attend_kernel(heads, groups, tokens, q_ref, *refs):
    count = len(refs) - 5
    shards = count // 2
    key_refs, value_refs = refs[:shards], refs[shards:count]
    out_ref, fq, fkv, keys, values = refs[count:]
    d = q_ref.shape[1]
    reach = (shards - 1) * tokens
    ratio = heads // groups
    g = pl.program_id(0)

    @pl.when(g == 0)
    def _():
        fq[...] = q_ref[...].astype(F32)
        for s in range(shards):
            fkv[0, pl.ds(s * tokens * groups, tokens * groups), :] = key_refs[s][...].astype(F32)
            fkv[1, pl.ds(s * tokens * groups, tokens * groups), :] = value_refs[s][...].astype(F32)
        values[:, d:] = jnp.ones((values.shape[0], d), BF16)

    span = reach + tokens
    keys[...] = fkv[0, pl.ds(g, span, stride=groups), :].astype(BF16)
    values[:, :d] = fkv[1, pl.ds(g, span, stride=groups), :].astype(BF16)
    width = WINDOW + ROWS
    anchor = lax.axis_index("ctx") * tokens
    row = lax.broadcasted_iota(jnp.int32, (ROWS, ROWS), 0)
    col = lax.broadcasted_iota(jnp.int32, (ROWS, ROWS), 1)
    lane = lax.broadcasted_iota(jnp.int32, (1, width), 1)
    low = jnp.where(col > row, 0.0, -jnp.inf)
    high = jnp.where(col <= row, 0.0, -jnp.inf)
    factor = math.log2(math.e) / math.sqrt(d)
    for b in range(tokens // ROWS):
        start = reach - WINDOW + b * ROWS
        key_part = keys[start : start + width, :]
        value_part = values[start : start + width, :]
        exists = jnp.where(lane + (anchor - reach + start) >= 0, 0.0, -jnp.inf)
        for r in range(ratio):
            h = g * ratio + r
            q = fq[pl.ds(b * ROWS * heads + h, ROWS, stride=heads), :].astype(BF16)
            scores = dot_nt(q, key_part) + exists
            scores = jnp.concatenate(
                (scores[:, :ROWS] + low, scores[:, ROWS:WINDOW], scores[:, WINDOW:] + high), axis=1
            )
            top = jnp.max(scores, axis=1, keepdims=True)
            weights = jnp.exp2((scores - top) * factor).astype(BF16)
            mixed = dot(weights, value_part)
            out_ref[b * ROWS : (b + 1) * ROWS, r * d : (r + 1) * d] = (mixed[:, :d] / mixed[:, d:]).astype(BF16)


def attend(q, key_shards, value_shards):
    tokens, heads, d = q.shape
    groups = key_shards[0].shape[1]
    shards = len(key_shards)
    flat = [x.reshape(-1, d) for x in (q, *key_shards, *value_shards)]
    span = shards * tokens
    return pl.pallas_call(
        functools.partial(attend_kernel, heads, groups, tokens),
        grid=(groups,),
        in_specs=[pl.BlockSpec(x.shape, lambda g: (0, 0)) for x in flat],
        out_specs=pl.BlockSpec((tokens, heads // groups * d), lambda g: (0, g)),
        out_shape=jax.ShapeDtypeStruct((tokens, heads * d), BF16),
        scratch_shapes=[
            pltpu.VMEM((tokens * heads, d), F32),
            pltpu.VMEM((2, span * groups, d), F32),
            pltpu.VMEM((span, d), BF16),
            pltpu.VMEM((span, 2 * d), BF16),
        ],
        compiler_params=pltpu.CompilerParams(vmem_limit_bytes=VMEM_BYTES),
        cost_estimate=pl.CostEstimate(flops=8_000_000_000, bytes_accessed=4_000_000, transcendentals=5_000_000),
        name="attend",
    )(*flat)


def shifted(block, distance):
    n = lax.axis_size("ctx")
    return lax.ppermute(block, "ctx", [(i, i + distance) for i in range(n - distance)])


def local(
    attn_query, attn_key, attention_value, delta_query, delta_key, delta_value, log_decay, beta_gate
):
    tokens = attn_query.shape[0]
    hops = -(-WINDOW // tokens)
    keys = [shifted(attn_key, s) for s in range(hops, 0, -1)] + [attn_key]
    values = [shifted(attention_value, s) for s in range(hops, 0, -1)] + [attention_value]
    moved, local_part, pairs = delta_local(delta_query, delta_key, delta_value, log_decay, beta_gate)
    states = incoming_states(pairs)
    attn_local = attend(attn_query, keys, values)
    attn_out = lax.all_to_all(attn_local, "head", split_axis=0, concat_axis=1, tiled=True)
    delta = delta_final(moved, local_part, states)
    delta_out = lax.all_to_all(delta, "head", split_axis=0, concat_axis=1, tiled=True)
    return (attn_out, delta_out)


def solution(mesh):
    placed = (P("ctx", "head", None),) * 6 + (P("head", "ctx"),) * 2
    return jax.shard_map(
        local,
        mesh=mesh,
        in_specs=placed,
        out_specs=(P(("ctx", "head"), None), P(("ctx", "head"), None)),
        check_vma=False,
    )
```

```python
import functools
import math

import jax
import jax.numpy as jnp
from jax import lax
from jax.experimental import pallas as pl
from jax.experimental.pallas import tpu as pltpu
from jax.sharding import PartitionSpec as P

WINDOW = 1024
CHUNK = 128
PAIR = 2
norm_epsilon = 1e-06
F32, BF16 = jnp.float32, jnp.bfloat16
VMEM_BYTES = 56 * 1024 * 1024


def dot(a, b):
    return lax.dot_general(a, b, (((1,), (0,)), ((), ())), preferred_element_type=F32)


def dot_nt(a, b):
    return lax.dot_general(a, b, (((1,), (1,)), ((), ())), preferred_element_type=F32)


def split(x):
    high = x.astype(BF16)
    return high, (x - high.astype(F32)).astype(BF16)


def dot_square(a, b):
    ah, al = split(a)
    bh, bl = split(b)
    right = jnp.concatenate((bh, bl), axis=1)
    both = dot(jnp.concatenate((ah, al), axis=1), jnp.concatenate((right, right), axis=0))
    width = b.shape[1]
    return both[:, :width] + both[:, width:]


def dot_wide(a, b):
    ah, al = split(a)
    bh, bl = split(b)
    return dot(jnp.concatenate((ah, al), axis=1), jnp.concatenate((bh, bh), axis=0)) + dot(ah, bl)


def row_cumsum(row, upper):
    a = row.astype(BF16)
    rest = row - a.astype(F32)
    b = rest.astype(BF16)
    c = (rest - b.astype(F32)).astype(BF16)
    return dot(a, upper) + (dot(b, upper) + dot(c, upper))


def delta_spans(parts, head_dim):
    size = CHUNK
    row = lax.broadcasted_iota(jnp.int32, (size, size), 0)
    col = lax.broadcasted_iota(jnp.int32, (size, size), 1)
    upper = (row <= col).astype(BF16)
    eye = (row == col).astype(F32)
    state = []
    for q, k, v, log_row, beta_row in parts:
        qb, kb = q.astype(BF16), k.astype(BF16)
        rk = lax.rsqrt(jnp.sum(k * k, axis=1, keepdims=True) + norm_epsilon)
        rq = lax.rsqrt(jnp.sum(q * q, axis=1, keepdims=True) + norm_epsilon) / math.sqrt(head_dim)
        g = row_cumsum(jnp.broadcast_to(log_row, (8, size)), upper)[0:1, :]
        g_row = jnp.broadcast_to(g, (size, size))
        g_col = g_row.T
        b_col = jnp.broadcast_to(beta_row, (size, size)).T
        rk_row = jnp.broadcast_to(rk, (size, size)).T
        ratio = jnp.exp(jnp.where(row >= col, g_col - g_row, -jnp.inf)) * rk_row
        strict = jnp.where(row > col, b_col * rk * ratio * dot_nt(kb, kb), 0.0)
        causal = rq * ratio * dot_nt(qb, kb)
        state.append((strict, causal, g_col, b_col, rk, rq, g))
    inverse = []
    first = (row // 2 == col // 2) & (row > col)
    for s in state:
        inverse.append(eye - jnp.where(first, s[0], 0.0))
    block = 2
    while block < size:
        mask = (row // (2 * block) == col // (2 * block)) & (row // block > col // block)
        half = [dot_square(t, jnp.where(mask, s[0], 0.0)) for t, s in zip(inverse, state)]
        inverse = [t - dot_square(x, t) for t, x in zip(inverse, half)]
        block *= 2
    out = []
    for (q, k, v, _, _), t, (strict, causal, g_col, b_col, rk, rq, g) in zip(parts, inverse, state):
        lead = jnp.exp(g_col)
        weighted = dot_wide(t, jnp.concatenate((b_col * lead * rk * k, b_col * v), axis=1))
        mixed = dot_wide(causal, weighted)
        queries = lead * rq * q - mixed[:, :head_dim]
        last = g[:, size - 1 : size]
        trail = jnp.exp(last - g_col) * rk
        th, tl = split(jnp.concatenate((trail, trail), axis=1) * weighted)
        kt = k.T.astype(BF16)
        written = dot(jnp.concatenate((kt, kt), axis=1), jnp.concatenate((th, tl), axis=0))
        out.append((queries, mixed[:, head_dim:], jnp.exp(last), written))
    return out


def compose(spans, head_dim):
    zeros = jnp.zeros((head_dim, head_dim), F32)
    r = lax.broadcasted_iota(jnp.int32, (head_dim, head_dim), 0)
    c = lax.broadcasted_iota(jnp.int32, (head_dim, head_dim), 1)
    eye = (r == c).astype(F32)
    carried, results = None, []
    for queries, mixed, keep, written in spans:
        if carried is None:
            results.append((queries, mixed))
            carried = jnp.concatenate((keep * eye - written[:, :head_dim], written[:, head_dim:]), axis=1)
        else:
            both = dot_wide(queries, carried)
            results.append((both[:, :head_dim], both[:, head_dim:] + mixed))
            step = dot_wide(written[:, :head_dim], carried)
            carried = keep * carried - step + jnp.concatenate((zeros, written[:, head_dim:]), axis=1)
    return results, carried


def delta_kernel(heads, tokens, q_ref, k_ref, v_ref, log_ref, beta_ref, moved_ref, local_ref, pair_ref, fq, fk, fv):
    head_dim = q_ref.shape[1]

    @pl.when(pl.program_id(0) == 0)
    def _():
        fq[...] = q_ref[...].astype(F32)
        fk[...] = k_ref[...].astype(F32)
        fv[...] = v_ref[...].astype(F32)

    count = tokens // CHUNK
    parts = []
    for j in range(PAIR):
        h = pl.program_id(0) * PAIR + j
        for c in range(count):
            rows = pl.ds(c * CHUNK * heads + h, CHUNK, stride=heads)
            lanes = slice(c * CHUNK, (c + 1) * CHUNK)
            pick = lax.broadcasted_iota(jnp.int32, (heads, CHUNK), 0) == h
            gates = [
                jnp.sum(jnp.where(pick, ref[:, lanes], 0.0), axis=0, keepdims=True) for ref in (log_ref, beta_ref)
            ]
            parts.append((fq[rows, :], fk[rows, :], fv[rows, :], *gates))
    spans = delta_spans(parts, head_dim)
    for j in range(PAIR):
        results, carried = compose(spans[j * count : (j + 1) * count], head_dim)
        for c, (moved, local_part) in enumerate(results):
            moved_ref[j, c * CHUNK : (c + 1) * CHUNK, :] = moved
            local_ref[j, c * CHUNK : (c + 1) * CHUNK, :] = local_part
        pair_ref[j] = carried.astype(pair_ref.dtype)


def delta_local(q, k, v, log_decay, beta):
    tokens, heads, d = q.shape
    flat = [x.reshape(tokens * heads, d) for x in (q, k, v)]
    full = pl.BlockSpec((tokens * heads, d), lambda i: (0, 0))
    gate = pl.BlockSpec((heads, tokens), lambda i: (0, 0))
    per_head = pl.BlockSpec((PAIR, tokens, d), lambda i: (i, 0, 0))
    return pl.pallas_call(
        functools.partial(delta_kernel, heads, tokens),
        grid=(heads // PAIR,),
        in_specs=[full, full, full, gate, gate],
        out_specs=[per_head, per_head, pl.BlockSpec((PAIR, d, 2 * d), lambda i: (i, 0, 0))],
        out_shape=[
            jax.ShapeDtypeStruct((heads, tokens, d), F32),
            jax.ShapeDtypeStruct((heads, tokens, d), F32),
            jax.ShapeDtypeStruct((heads, d, 2 * d), BF16),
        ],
        scratch_shapes=[pltpu.VMEM((tokens * heads, d), F32)] * 3,
        compiler_params=pltpu.CompilerParams(vmem_limit_bytes=VMEM_BYTES),
        cost_estimate=pl.CostEstimate(flops=10_000_000_000, bytes_accessed=8_000_000, transcendentals=0),
        name="delta_local",
    )(*flat, log_decay, beta)


def prefix_kernel(pair_ref, state_ref):
    n, d = pair_ref.shape[0], pair_ref.shape[1]
    state = jnp.zeros((d, d), F32)
    for i in range(n):
        state_ref[i] = state.astype(state_ref.dtype)
        if i < n - 1:
            sh, sl = split(state)
            move = pair_ref[i, :, :d]
            both = dot(jnp.concatenate((move, move), axis=1), jnp.concatenate((sh, sl), axis=0))
            state = both + pair_ref[i, :, d:].astype(F32)


def final_kernel(moved_ref, local_ref, state_ref, out_ref):
    sh = state_ref[0]
    mh, ml = split(moved_ref[0])
    both = dot(jnp.concatenate((mh, ml), axis=1), jnp.concatenate((sh, sh), axis=0))
    out_ref[...] = (both + local_ref[0]).astype(BF16)


def delta_final(moved, local_part, states):
    heads, tokens, d = moved.shape
    per_head = pl.BlockSpec((1, tokens, d), lambda h: (h, 0, 0))
    return pl.pallas_call(
        final_kernel,
        grid=(heads,),
        in_specs=[per_head, per_head, pl.BlockSpec((1, d, d), lambda h: (h, 0, 0))],
        out_specs=pl.BlockSpec((tokens, d), lambda h: (0, h)),
        out_shape=jax.ShapeDtypeStruct((tokens, heads * d), BF16),
        compiler_params=pltpu.CompilerParams(vmem_limit_bytes=VMEM_BYTES),
        cost_estimate=pl.CostEstimate(flops=2_000_000_000, bytes_accessed=6_000_000, transcendentals=0),
        name="delta_final",
    )(moved, local_part, states)


def incoming_states(pairs):
    heads, d = pairs.shape[0], pairs.shape[1]
    n = lax.axis_size("ctx")
    if n == heads:
        mine = lax.all_to_all(pairs, "ctx", split_axis=0, concat_axis=0, tiled=True)
        states = pl.pallas_call(
            prefix_kernel,
            out_shape=jax.ShapeDtypeStruct((n, d, d), BF16),
            cost_estimate=pl.CostEstimate(flops=500_000_000, bytes_accessed=800_000, transcendentals=0),
            name="prefix",
        )(mine)
        return lax.all_to_all(states, "ctx", split_axis=0, concat_axis=0, tiled=True)
    transit, source = pairs[:, :, :d].astype(F32), pairs[:, :, d:].astype(F32)

    def relay(turn, inbound):
        leaving = jnp.einsum("hij,hjk->hik", transit, inbound, precision=lax.Precision.HIGHEST) + source
        return lax.ppermute(leaving, "ctx", [(i, i + 1) for i in range(n - 1)])

    return lax.fori_loop(0, n - 1, relay, jnp.zeros((heads, d, d), F32)).astype(BF16)


ROWS = 128


def attend_kernel(heads, groups, tokens, q_ref, *refs):
    count = len(refs) - 5
    shards = count // 2
    key_refs, value_refs = refs[:shards], refs[shards:count]
    out_ref, fq, fkv, keys, values = refs[count:]
    d = q_ref.shape[1]
    reach = (shards - 1) * tokens
    ratio = heads // groups
    g = pl.program_id(0)

    @pl.when(g == 0)
    def _():
        fq[...] = q_ref[...].astype(F32)
        for s in range(shards):
            fkv[0, pl.ds(s * tokens * groups, tokens * groups), :] = key_refs[s][...].astype(F32)
            fkv[1, pl.ds(s * tokens * groups, tokens * groups), :] = value_refs[s][...].astype(F32)
        values[:, d:] = jnp.ones((values.shape[0], d), BF16)

    span = reach + tokens
    keys[...] = fkv[0, pl.ds(g, span, stride=groups), :].astype(BF16)
    values[:, :d] = fkv[1, pl.ds(g, span, stride=groups), :].astype(BF16)
    width = WINDOW + ROWS
    anchor = lax.axis_index("ctx") * tokens
    row = lax.broadcasted_iota(jnp.int32, (ROWS, ROWS), 0)
    col = lax.broadcasted_iota(jnp.int32, (ROWS, ROWS), 1)
    lane = lax.broadcasted_iota(jnp.int32, (1, width), 1)
    low = jnp.where(col > row, 0.0, -jnp.inf)
    high = jnp.where(col <= row, 0.0, -jnp.inf)
    factor = math.log2(math.e) / math.sqrt(d)
    for b in range(tokens // ROWS):
        start = reach - WINDOW + b * ROWS
        key_part = keys[start : start + width, :]
        value_part = values[start : start + width, :]
        exists = jnp.where(lane + (anchor - reach + start) >= 0, 0.0, -jnp.inf)
        for r in range(ratio):
            h = g * ratio + r
            q = fq[pl.ds(b * ROWS * heads + h, ROWS, stride=heads), :].astype(BF16)
            scores = dot_nt(q, key_part) + exists
            scores = jnp.concatenate(
                (scores[:, :ROWS] + low, scores[:, ROWS:WINDOW], scores[:, WINDOW:] + high), axis=1
            )
            top = jnp.max(scores, axis=1, keepdims=True)
            weights = jnp.exp2((scores - top) * factor).astype(BF16)
            mixed = dot(weights, value_part)
            out_ref[b * ROWS : (b + 1) * ROWS, r * d : (r + 1) * d] = (mixed[:, :d] / mixed[:, d:]).astype(BF16)


def attend(q, key_shards, value_shards):
    tokens, heads, d = q.shape
    groups = key_shards[0].shape[1]
    shards = len(key_shards)
    flat = [x.reshape(-1, d) for x in (q, *key_shards, *value_shards)]
    span = shards * tokens
    return pl.pallas_call(
        functools.partial(attend_kernel, heads, groups, tokens),
        grid=(groups,),
        in_specs=[pl.BlockSpec(x.shape, lambda g: (0, 0)) for x in flat],
        out_specs=pl.BlockSpec((tokens, heads // groups * d), lambda g: (0, g)),
        out_shape=jax.ShapeDtypeStruct((tokens, heads * d), BF16),
        scratch_shapes=[
            pltpu.VMEM((tokens * heads, d), F32),
            pltpu.VMEM((2, span * groups, d), F32),
            pltpu.VMEM((span, d), BF16),
            pltpu.VMEM((span, 2 * d), BF16),
        ],
        compiler_params=pltpu.CompilerParams(vmem_limit_bytes=VMEM_BYTES),
        cost_estimate=pl.CostEstimate(flops=8_000_000_000, bytes_accessed=4_000_000, transcendentals=5_000_000),
        name="attend",
    )(*flat)


def attend_rows(q, key_part, value_part, exists, low, high, factor):
    d = q.shape[1]
    scores = dot_nt(q, key_part) + exists
    scores = jnp.concatenate((scores[:, :ROWS] + low, scores[:, ROWS:WINDOW], scores[:, WINDOW:] + high), axis=1)
    top = jnp.max(scores, axis=1, keepdims=True)
    weights = jnp.exp2((scores - top) * factor).astype(BF16)
    mixed = dot(weights, value_part)
    return (mixed[:, :d] / mixed[:, d:]).astype(BF16)


def fused_kernel(n, heads, groups, tokens, shards, q_ref, *refs):
    key_refs, value_refs = refs[:shards], refs[shards : 2 * shards]
    moved_ref, local_ref, pair_ref, attn_ref, delta_ref = refs[2 * shards : 2 * shards + 5]
    (fq, fkv, keys, values, moved, local_part, mine, states, incoming, attn_stage, delta_stage) = refs[2 * shards + 5 : 2 * shards + 16]
    (load_sem, own_sem, attn_send, attn_recv, delta_send, delta_recv, go_send, go_recv, back_send, back_recv) = refs[2 * shards + 16 :]
    d = q_ref.shape[1]
    ratio = heads // groups
    reach = (shards - 1) * tokens
    span = reach + tokens
    width = WINDOW + ROWS
    team = tokens // ROWS
    ctx, head = lax.axis_index("ctx"), lax.axis_index("head")

    barrier = pltpu.get_barrier_semaphore()
    for o in range(1, n):
        pl.semaphore_signal(barrier, inc=1, device_id={"ctx": lax.rem(ctx + o, n)}, device_id_type=pl.DeviceIdType.MESH)
    for o in range(1, team):
        pl.semaphore_signal(barrier, inc=1, device_id={"head": lax.rem(head + o, team)}, device_id_type=pl.DeviceIdType.MESH)
    loads = [
        pltpu.make_async_copy(moved_ref, moved, load_sem.at[0]),
        pltpu.make_async_copy(local_ref, local_part, load_sem.at[1]),
    ]
    for load in loads:
        load.start()
    fq[...] = q_ref[...].astype(F32)
    for s in range(shards):
        rows = pl.ds(s * tokens * groups, tokens * groups)
        fkv[0, rows, :] = key_refs[s][...].astype(F32)
        fkv[1, rows, :] = value_refs[s][...].astype(F32)
    values[:, d:] = jnp.ones((span, d), BF16)
    pl.semaphore_wait(barrier, n - 1 + team - 1)

    def remote(src, dst, send, recv, where):
        return pltpu.make_async_remote_copy(
            src_ref=src, dst_ref=dst, send_sem=send, recv_sem=recv, device_id=where,
            device_id_type=pl.DeviceIdType.MESH,
        )

    def go(o, slot):
        to = lax.rem(ctx + o, n)
        return remote(pair_ref.at[to], mine.at[slot], go_send.at[o - 1], go_recv.at[o - 1], {"ctx": to})

    def back(o, slot):
        to = lax.rem(ctx + o, n)
        return remote(states.at[to], incoming.at[slot], back_send.at[o - 1], back_recv.at[o - 1], {"ctx": to})

    for o in range(1, n):
        go(o, ctx).start()
    mine[ctx] = pair_ref[ctx]

    anchor = ctx * tokens
    row = lax.broadcasted_iota(jnp.int32, (ROWS, ROWS), 0)
    col = lax.broadcasted_iota(jnp.int32, (ROWS, ROWS), 1)
    lane = lax.broadcasted_iota(jnp.int32, (1, width), 1)
    low = jnp.where(col > row, 0.0, -jnp.inf)
    high = jnp.where(col <= row, 0.0, -jnp.inf)
    factor = math.log2(math.e) / math.sqrt(d)
    offsets = list(range(1, team)) + [0]

    def attn_copy(g, o, owner):
        to = lax.rem(head + o, team)
        place = attn_ref.at[:, pl.ds(pl.multiple_of((owner * groups + g) * ratio * d, ratio * d), ratio * d)]
        if o == 0:
            return pltpu.make_async_copy(attn_stage.at[g, o], place, own_sem.at[g])
        return remote(attn_stage.at[g, o], place, attn_send.at[g, o - 1], attn_recv.at[g, o - 1], {"head": to})

    def one_group(g, _):
        keys[...] = fkv[0, pl.ds(g, span, stride=groups), :].astype(BF16)
        values[:, :d] = fkv[1, pl.ds(g, span, stride=groups), :].astype(BF16)
        for o in offsets:
            b = lax.rem(head + o, team)
            start = pl.multiple_of(reach - WINDOW + b * ROWS, ROWS)
            key_part = keys[pl.ds(start, width), :]
            value_part = values[pl.ds(start, width), :]
            exists = jnp.where(lane + (anchor - reach + start) >= 0, 0.0, -jnp.inf)
            for r in range(ratio):
                q = fq[pl.ds(b * ROWS * heads + g * ratio + r, ROWS, stride=heads), :].astype(BF16)
                attn_stage[g, o, :, r * d : (r + 1) * d] = attend_rows(
                    q, key_part, value_part, exists, low, high, factor
                )
            attn_copy(g, o, head).start()
        return 0

    lax.fori_loop(0, groups, one_group, 0)

    for o in range(1, n):
        go(o, lax.rem(ctx - o + n, n)).wait_recv()
    state = jnp.zeros((d, d), F32)
    for i in range(n):
        states[i] = state.astype(BF16)
        if i < n - 1:
            sh, sl = split(state)
            move = mine[i, :, :d]
            both = dot(jnp.concatenate((move, move), axis=1), jnp.concatenate((sh, sl), axis=0))
            state = both + mine[i, :, d:].astype(F32)
    for o in range(1, n):
        back(o, ctx).start()
    incoming[ctx] = states[ctx]
    for load in loads:
        load.wait()
    for o in range(1, n):
        back(o, lax.rem(ctx - o + n, n)).wait_recv()

    def delta_copy(o, owner):
        to = lax.rem(head + o, team)
        place = delta_ref.at[:, pl.ds(pl.multiple_of(owner * heads * d, heads * d), heads * d)]
        if o == 0:
            return pltpu.make_async_copy(delta_stage.at[o], place, own_sem.at[groups])
        return remote(delta_stage.at[o], place, delta_send.at[o - 1], delta_recv.at[o - 1], {"head": to})

    for o in offsets:
        rows = pl.ds(pl.multiple_of(lax.rem(head + o, team) * ROWS, ROWS), ROWS)
        for h in range(heads):
            mh, ml = split(moved[h, rows, :])
            sh = incoming[h]
            both = dot(jnp.concatenate((mh, ml), axis=1), jnp.concatenate((sh, sh), axis=0))
            delta_stage[o, :, h * d : (h + 1) * d] = (both + local_part[h, rows, :]).astype(BF16)
        delta_copy(o, head).start()

    for g in range(groups):
        attn_copy(g, 0, head).wait()
        for o in range(1, team):
            attn_copy(g, o, head).wait_send()
            attn_copy(g, o, lax.rem(head - o + team, team)).wait_recv()
    delta_copy(0, head).wait()
    for o in range(1, team):
        delta_copy(o, head).wait_send()
        delta_copy(o, lax.rem(head - o + team, team)).wait_recv()
    for o in range(1, n):
        go(o, ctx).wait_send()
        back(o, ctx).wait_send()


def fused(q, key_shards, value_shards, moved, local_part, pairs):
    tokens, heads, d = q.shape
    groups = key_shards[0].shape[1]
    shards = len(key_shards)
    n, team = lax.axis_size("ctx"), lax.axis_size("head")
    flat = [x.reshape(-1, d) for x in (q, *key_shards, *value_shards)]
    span = shards * tokens
    vmem, anywhere = pl.BlockSpec(memory_space=pltpu.VMEM), pl.BlockSpec(memory_space=pl.ANY)
    result = jax.ShapeDtypeStruct((ROWS, team * heads * d), BF16)
    sems = pltpu.SemaphoreType.DMA
    return pl.pallas_call(
        functools.partial(fused_kernel, n, heads, groups, tokens, shards),
        in_specs=[vmem] * len(flat) + [anywhere, anywhere, vmem],
        out_specs=[anywhere, anywhere],
        out_shape=[result, result],
        scratch_shapes=[
            pltpu.VMEM((tokens * heads, d), F32),
            pltpu.VMEM((2, span * groups, d), F32),
            pltpu.VMEM((span, d), BF16),
            pltpu.VMEM((span, 2 * d), BF16),
            pltpu.VMEM(moved.shape, F32),
            pltpu.VMEM(local_part.shape, F32),
            pltpu.VMEM((n, d, 2 * d), BF16),
            pltpu.VMEM((n, d, d), BF16),
            pltpu.VMEM((heads, d, d), BF16),
            pltpu.VMEM((groups, team, ROWS, heads // groups * d), BF16),
            pltpu.VMEM((team, ROWS, heads * d), BF16),
            sems((2,)),
            sems((groups + 1,)),
            sems((groups, team - 1)),
            sems((groups, team - 1)),
            sems((team - 1,)),
            sems((team - 1,)),
            sems((n - 1,)),
            sems((n - 1,)),
            sems((n - 1,)),
            sems((n - 1,)),
        ],
        compiler_params=pltpu.CompilerParams(
            vmem_limit_bytes=VMEM_BYTES, collective_id=1, has_side_effects=True
        ),
        cost_estimate=pl.CostEstimate(flops=10_000_000_000, bytes_accessed=12_000_000, transcendentals=5_000_000),
        name="attend_and_exchange",
    )(*flat, moved, local_part, pairs)


def shifted(block, distance):
    n = lax.axis_size("ctx")
    return lax.ppermute(block, "ctx", [(i, i + distance) for i in range(n - distance)])


def local(
    attn_query, attn_key, attention_value, delta_query, delta_key, delta_value, log_decay, beta_gate
):
    tokens = attn_query.shape[0]
    hops = -(-WINDOW // tokens)
    keys = [shifted(attn_key, s) for s in range(hops, 0, -1)] + [attn_key]
    values = [shifted(attention_value, s) for s in range(hops, 0, -1)] + [attention_value]
    moved, local_part, pairs = delta_local(delta_query, delta_key, delta_value, log_decay, beta_gate)
    heads, team = attn_query.shape[1], lax.axis_size("head")
    if lax.axis_size("ctx") == heads and tokens == team * ROWS:
        return tuple(fused(attn_query, keys, values, moved, local_part, pairs))
    states = incoming_states(pairs)
    attn_local = attend(attn_query, keys, values)
    attn_out = lax.all_to_all(attn_local, "head", split_axis=0, concat_axis=1, tiled=True)
    delta = delta_final(moved, local_part, states)
    delta_out = lax.all_to_all(delta, "head", split_axis=0, concat_axis=1, tiled=True)
    return (attn_out, delta_out)


def solution(mesh):
    placed = (P("ctx", "head", None),) * 6 + (P("head", "ctx"),) * 2
    return jax.shard_map(
        local,
        mesh=mesh,
        in_specs=placed,
        out_specs=(P(("ctx", "head"), None), P(("ctx", "head"), None)),
        check_vma=False,
    )
```

```python
import functools
import math

import jax
import jax.numpy as jnp
from jax import lax
from jax.experimental import pallas as pl
from jax.experimental.pallas import tpu as pltpu
from jax.sharding import PartitionSpec as P

WINDOW = 1024
CHUNK = 128
PAIR = 2
norm_epsilon = 1e-06
F32, BF16 = jnp.float32, jnp.bfloat16
VMEM_BYTES = 56 * 1024 * 1024


def dot(a, b):
    return lax.dot_general(a, b, (((1,), (0,)), ((), ())), preferred_element_type=F32)


def dot_nt(a, b):
    return lax.dot_general(a, b, (((1,), (1,)), ((), ())), preferred_element_type=F32)


def split(x):
    high = x.astype(BF16)
    return high, (x - high.astype(F32)).astype(BF16)


def dot_square(a, b):
    ah, al = split(a)
    bh, bl = split(b)
    right = jnp.concatenate((bh, bl), axis=1)
    both = dot(jnp.concatenate((ah, al), axis=1), jnp.concatenate((right, right), axis=0))
    width = b.shape[1]
    return both[:, :width] + both[:, width:]


def dot_wide(a, b):
    ah, al = split(a)
    bh, bl = split(b)
    return dot(jnp.concatenate((ah, al), axis=1), jnp.concatenate((bh, bh), axis=0)) + dot(ah, bl)


def row_cumsum(row, upper):
    a = row.astype(BF16)
    rest = row - a.astype(F32)
    b = rest.astype(BF16)
    c = (rest - b.astype(F32)).astype(BF16)
    return dot(a, upper) + (dot(b, upper) + dot(c, upper))


def delta_spans(parts, head_dim):
    size = CHUNK
    row = lax.broadcasted_iota(jnp.int32, (size, size), 0)
    col = lax.broadcasted_iota(jnp.int32, (size, size), 1)
    upper = (row <= col).astype(BF16)
    eye = (row == col).astype(F32)
    state = []
    for q, k, v, log_row, beta_row in parts:
        qb, kb = q.astype(BF16), k.astype(BF16)
        rk = lax.rsqrt(jnp.sum(k * k, axis=1, keepdims=True) + norm_epsilon)
        rq = lax.rsqrt(jnp.sum(q * q, axis=1, keepdims=True) + norm_epsilon) / math.sqrt(head_dim)
        g = row_cumsum(jnp.broadcast_to(log_row, (8, size)), upper)[0:1, :]
        g_row = jnp.broadcast_to(g, (size, size))
        g_col = g_row.T
        b_col = jnp.broadcast_to(beta_row, (size, size)).T
        rk_row = jnp.broadcast_to(rk, (size, size)).T
        ratio = jnp.exp(jnp.where(row >= col, g_col - g_row, -jnp.inf)) * rk_row
        strict = jnp.where(row > col, b_col * rk * ratio * dot_nt(kb, kb), 0.0)
        causal = rq * ratio * dot_nt(qb, kb)
        state.append((strict, causal, g_col, b_col, rk, rq, g))
    inverse = []
    first = (row // 2 == col // 2) & (row > col)
    for s in state:
        inverse.append(eye - jnp.where(first, s[0], 0.0))
    block = 2
    while block < size:
        mask = (row // (2 * block) == col // (2 * block)) & (row // block > col // block)
        half = [dot_square(t, jnp.where(mask, s[0], 0.0)) for t, s in zip(inverse, state)]
        inverse = [t - dot_square(x, t) for t, x in zip(inverse, half)]
        block *= 2
    out = []
    for (q, k, v, _, _), t, (strict, causal, g_col, b_col, rk, rq, g) in zip(parts, inverse, state):
        lead = jnp.exp(g_col)
        weighted = dot_wide(t, jnp.concatenate((b_col * lead * rk * k, b_col * v), axis=1))
        mixed = dot_wide(causal, weighted)
        queries = lead * rq * q - mixed[:, :head_dim]
        last = g[:, size - 1 : size]
        trail = jnp.exp(last - g_col) * rk
        th, tl = split(jnp.concatenate((trail, trail), axis=1) * weighted)
        kt = k.T.astype(BF16)
        written = dot(jnp.concatenate((kt, kt), axis=1), jnp.concatenate((th, tl), axis=0))
        out.append((queries, mixed[:, head_dim:], jnp.exp(last), written))
    return out


def compose(spans, head_dim):
    zeros = jnp.zeros((head_dim, head_dim), F32)
    r = lax.broadcasted_iota(jnp.int32, (head_dim, head_dim), 0)
    c = lax.broadcasted_iota(jnp.int32, (head_dim, head_dim), 1)
    eye = (r == c).astype(F32)
    carried, results = None, []
    for queries, mixed, keep, written in spans:
        if carried is None:
            results.append((queries, mixed))
            carried = jnp.concatenate((keep * eye - written[:, :head_dim], written[:, head_dim:]), axis=1)
        else:
            both = dot_wide(queries, carried)
            results.append((both[:, :head_dim], both[:, head_dim:] + mixed))
            step = dot_wide(written[:, :head_dim], carried)
            carried = keep * carried - step + jnp.concatenate((zeros, written[:, head_dim:]), axis=1)
    return results, carried


def delta_kernel(heads, tokens, q_ref, k_ref, v_ref, log_ref, beta_ref, moved_ref, local_ref, pair_ref, fq, fk, fv):
    head_dim = q_ref.shape[1]

    @pl.when(pl.program_id(0) == 0)
    def _():
        fq[...] = q_ref[...].astype(F32)
        fk[...] = k_ref[...].astype(F32)
        fv[...] = v_ref[...].astype(F32)

    count = tokens // CHUNK
    parts = []
    for j in range(PAIR):
        h = pl.program_id(0) * PAIR + j
        for c in range(count):
            rows = pl.ds(c * CHUNK * heads + h, CHUNK, stride=heads)
            lanes = slice(c * CHUNK, (c + 1) * CHUNK)
            pick = lax.broadcasted_iota(jnp.int32, (heads, CHUNK), 0) == h
            gates = [
                jnp.sum(jnp.where(pick, ref[:, lanes], 0.0), axis=0, keepdims=True) for ref in (log_ref, beta_ref)
            ]
            parts.append((fq[rows, :], fk[rows, :], fv[rows, :], *gates))
    spans = delta_spans(parts, head_dim)
    for j in range(PAIR):
        results, carried = compose(spans[j * count : (j + 1) * count], head_dim)
        for c, (moved, local_part) in enumerate(results):
            moved_ref[j, c * CHUNK : (c + 1) * CHUNK, :] = moved
            local_ref[j, c * CHUNK : (c + 1) * CHUNK, :] = local_part
        pair_ref[j] = carried.astype(pair_ref.dtype)


def delta_local(q, k, v, log_decay, beta):
    tokens, heads, d = q.shape
    flat = [x.reshape(tokens * heads, d) for x in (q, k, v)]
    full = pl.BlockSpec((tokens * heads, d), lambda i: (0, 0))
    gate = pl.BlockSpec((heads, tokens), lambda i: (0, 0))
    per_head = pl.BlockSpec((PAIR, tokens, d), lambda i: (i, 0, 0))
    return pl.pallas_call(
        functools.partial(delta_kernel, heads, tokens),
        grid=(heads // PAIR,),
        in_specs=[full, full, full, gate, gate],
        out_specs=[per_head, per_head, pl.BlockSpec((PAIR, d, 2 * d), lambda i: (i, 0, 0))],
        out_shape=[
            jax.ShapeDtypeStruct((heads, tokens, d), F32),
            jax.ShapeDtypeStruct((heads, tokens, d), F32),
            jax.ShapeDtypeStruct((heads, d, 2 * d), BF16),
        ],
        scratch_shapes=[pltpu.VMEM((tokens * heads, d), F32)] * 3,
        compiler_params=pltpu.CompilerParams(vmem_limit_bytes=VMEM_BYTES),
        cost_estimate=pl.CostEstimate(flops=10_000_000_000, bytes_accessed=8_000_000, transcendentals=0),
        name="delta_local",
    )(*flat, log_decay, beta)


def prefix_kernel(pair_ref, state_ref):
    n, d = pair_ref.shape[0], pair_ref.shape[1]
    state = jnp.zeros((d, d), F32)
    for i in range(n):
        state_ref[i] = state.astype(state_ref.dtype)
        if i < n - 1:
            sh, sl = split(state)
            move = pair_ref[i, :, :d]
            both = dot(jnp.concatenate((move, move), axis=1), jnp.concatenate((sh, sl), axis=0))
            state = both + pair_ref[i, :, d:].astype(F32)


def final_kernel(moved_ref, local_ref, state_ref, out_ref):
    sh = state_ref[0]
    mh, ml = split(moved_ref[0])
    both = dot(jnp.concatenate((mh, ml), axis=1), jnp.concatenate((sh, sh), axis=0))
    out_ref[...] = (both + local_ref[0]).astype(BF16)


def delta_final(moved, local_part, states):
    heads, tokens, d = moved.shape
    per_head = pl.BlockSpec((1, tokens, d), lambda h: (h, 0, 0))
    return pl.pallas_call(
        final_kernel,
        grid=(heads,),
        in_specs=[per_head, per_head, pl.BlockSpec((1, d, d), lambda h: (h, 0, 0))],
        out_specs=pl.BlockSpec((tokens, d), lambda h: (0, h)),
        out_shape=jax.ShapeDtypeStruct((tokens, heads * d), BF16),
        compiler_params=pltpu.CompilerParams(vmem_limit_bytes=VMEM_BYTES),
        cost_estimate=pl.CostEstimate(flops=2_000_000_000, bytes_accessed=6_000_000, transcendentals=0),
        name="delta_final",
    )(moved, local_part, states)


def incoming_states(pairs):
    heads, d = pairs.shape[0], pairs.shape[1]
    n = lax.axis_size("ctx")
    if n == heads:
        mine = lax.all_to_all(pairs, "ctx", split_axis=0, concat_axis=0, tiled=True)
        states = pl.pallas_call(
            prefix_kernel,
            out_shape=jax.ShapeDtypeStruct((n, d, d), BF16),
            cost_estimate=pl.CostEstimate(flops=500_000_000, bytes_accessed=800_000, transcendentals=0),
            name="prefix",
        )(mine)
        return lax.all_to_all(states, "ctx", split_axis=0, concat_axis=0, tiled=True)
    transit, source = pairs[:, :, :d].astype(F32), pairs[:, :, d:].astype(F32)

    def relay(turn, inbound):
        leaving = jnp.einsum("hij,hjk->hik", transit, inbound, precision=lax.Precision.HIGHEST) + source
        return lax.ppermute(leaving, "ctx", [(i, i + 1) for i in range(n - 1)])

    return lax.fori_loop(0, n - 1, relay, jnp.zeros((heads, d, d), F32)).astype(BF16)


ROWS = 128


def attend_kernel(heads, groups, tokens, q_ref, *refs):
    count = len(refs) - 5
    shards = count // 2
    key_refs, value_refs = refs[:shards], refs[shards:count]
    out_ref, fq, fkv, keys, values = refs[count:]
    d = q_ref.shape[1]
    reach = (shards - 1) * tokens
    ratio = heads // groups
    g = pl.program_id(0)

    @pl.when(g == 0)
    def _():
        fq[...] = q_ref[...].astype(F32)
        for s in range(shards):
            fkv[0, pl.ds(s * tokens * groups, tokens * groups), :] = key_refs[s][...].astype(F32)
            fkv[1, pl.ds(s * tokens * groups, tokens * groups), :] = value_refs[s][...].astype(F32)
        values[:, d:] = jnp.ones((values.shape[0], d), BF16)

    span = reach + tokens
    keys[...] = fkv[0, pl.ds(g, span, stride=groups), :].astype(BF16)
    values[:, :d] = fkv[1, pl.ds(g, span, stride=groups), :].astype(BF16)
    width = WINDOW + ROWS
    anchor = lax.axis_index("ctx") * tokens
    row = lax.broadcasted_iota(jnp.int32, (ROWS, ROWS), 0)
    col = lax.broadcasted_iota(jnp.int32, (ROWS, ROWS), 1)
    lane = lax.broadcasted_iota(jnp.int32, (1, width), 1)
    low = jnp.where(col > row, 0.0, -jnp.inf)
    high = jnp.where(col <= row, 0.0, -jnp.inf)
    factor = math.log2(math.e) / math.sqrt(d)
    for b in range(tokens // ROWS):
        start = reach - WINDOW + b * ROWS
        key_part = keys[start : start + width, :]
        value_part = values[start : start + width, :]
        exists = jnp.where(lane + (anchor - reach + start) >= 0, 0.0, -jnp.inf)
        for r in range(ratio):
            h = g * ratio + r
            q = fq[pl.ds(b * ROWS * heads + h, ROWS, stride=heads), :].astype(BF16)
            scores = dot_nt(q, key_part) + exists
            scores = jnp.concatenate(
                (scores[:, :ROWS] + low, scores[:, ROWS:WINDOW], scores[:, WINDOW:] + high), axis=1
            )
            top = jnp.max(scores, axis=1, keepdims=True)
            weights = jnp.exp2((scores - top) * factor).astype(BF16)
            mixed = dot(weights, value_part)
            out_ref[b * ROWS : (b + 1) * ROWS, r * d : (r + 1) * d] = (mixed[:, :d] / mixed[:, d:]).astype(BF16)


def attend(q, key_shards, value_shards):
    tokens, heads, d = q.shape
    groups = key_shards[0].shape[1]
    shards = len(key_shards)
    flat = [x.reshape(-1, d) for x in (q, *key_shards, *value_shards)]
    span = shards * tokens
    return pl.pallas_call(
        functools.partial(attend_kernel, heads, groups, tokens),
        grid=(groups,),
        in_specs=[pl.BlockSpec(x.shape, lambda g: (0, 0)) for x in flat],
        out_specs=pl.BlockSpec((tokens, heads // groups * d), lambda g: (0, g)),
        out_shape=jax.ShapeDtypeStruct((tokens, heads * d), BF16),
        scratch_shapes=[
            pltpu.VMEM((tokens * heads, d), F32),
            pltpu.VMEM((2, span * groups, d), F32),
            pltpu.VMEM((span, d), BF16),
            pltpu.VMEM((span, 2 * d), BF16),
        ],
        compiler_params=pltpu.CompilerParams(vmem_limit_bytes=VMEM_BYTES),
        cost_estimate=pl.CostEstimate(flops=8_000_000_000, bytes_accessed=4_000_000, transcendentals=5_000_000),
        name="attend",
    )(*flat)


def attend_rows(q, key_part, value_part, exists, low, high, factor):
    d = q.shape[1]
    scores = dot_nt(q, key_part) + exists
    scores = jnp.concatenate((scores[:, :ROWS] + low, scores[:, ROWS:WINDOW], scores[:, WINDOW:] + high), axis=1)
    top = jnp.max(scores, axis=1, keepdims=True)
    weights = jnp.exp2((scores - top) * factor).astype(BF16)
    mixed = dot(weights, value_part)
    return (mixed[:, :d] / mixed[:, d:]).astype(BF16)


def fused_kernel(n, heads, groups, tokens, shards, *refs):
    q_ref, key_ref, value_ref, dq_ref, dk_ref, dv_ref, log_ref, beta_ref, attn_ref, delta_ref = refs[:10]
    halo, fq, fkv, keys, values, moved, local_part, pair_ref, mine, states, incoming, attn_stage, delta_stage = refs[10:23]
    dq, dk, dv = refs[23:26]
    halo_send, halo_recv, own_sem, attn_send, attn_recv, delta_send, delta_recv, go_send, go_recv, back_send, back_recv = refs[26:]
    d = q_ref.shape[1]
    ratio = heads // groups
    reach = (shards - 1) * tokens
    span = reach + tokens
    width = WINDOW + ROWS
    team = tokens // ROWS
    ctx, head = lax.axis_index("ctx"), lax.axis_index("head")

    barrier = pltpu.get_barrier_semaphore()
    for o in range(1, n):
        pl.semaphore_signal(barrier, inc=1, device_id={"ctx": lax.rem(ctx + o, n)}, device_id_type=pl.DeviceIdType.MESH)
    for o in range(1, team):
        pl.semaphore_signal(barrier, inc=1, device_id={"head": lax.rem(head + o, team)}, device_id_type=pl.DeviceIdType.MESH)
    pl.semaphore_wait(barrier, n - 1 + team - 1)

    def remote(src, dst, send, recv, where):
        return pltpu.make_async_remote_copy(
            src_ref=src, dst_ref=dst, send_sem=send, recv_sem=recv, device_id=where,
            device_id_type=pl.DeviceIdType.MESH,
        )

    def go(o, slot):
        to = lax.rem(ctx + o, n)
        return remote(pair_ref.at[to], mine.at[slot], go_send.at[o - 1], go_recv.at[o - 1], {"ctx": to})

    def back(o, slot):
        to = lax.rem(ctx + o, n)
        return remote(states.at[to], incoming.at[slot], back_send.at[o - 1], back_recv.at[o - 1], {"ctx": to})

    def halo_copy(o, side):
        source = (key_ref, value_ref)[side]
        return remote(
            source, halo.at[o - 1, side], halo_send.at[o - 1, side], halo_recv.at[o - 1, side],
            {"ctx": lax.rem(ctx + o, n)},
        )

    hops = shards - 1
    for o in range(1, shards):
        for side in range(2):
            halo_copy(o, side).start()
    dq[...] = dq_ref[...].astype(F32)
    dk[...] = dk_ref[...].astype(F32)
    dv[...] = dv_ref[...].astype(F32)

    def delta_pair(p, _):
        count = tokens // CHUNK
        parts = []
        for j in range(PAIR):
            h = p * PAIR + j
            pick = lax.broadcasted_iota(jnp.int32, (heads, CHUNK), 0) == h
            for c in range(count):
                rows = pl.ds(c * CHUNK * heads + h, CHUNK, stride=heads)
                lanes = slice(c * CHUNK, (c + 1) * CHUNK)
                gates = [
                    jnp.sum(jnp.where(pick, ref[:, lanes], 0.0), axis=0, keepdims=True)
                    for ref in (log_ref, beta_ref)
                ]
                parts.append((dq[rows, :], dk[rows, :], dv[rows, :], *gates))
        spans = delta_spans(parts, d)
        for j in range(PAIR):
            h = p * PAIR + j
            results, carried = compose(spans[j * count : (j + 1) * count], d)
            for c, (one, two) in enumerate(results):
                moved[h, c * CHUNK : (c + 1) * CHUNK, :] = one
                local_part[h, c * CHUNK : (c + 1) * CHUNK, :] = two
            pair_ref[h] = carried.astype(BF16)
        return 0

    def attention():
        fq[...] = q_ref[...].astype(F32)
        own = pl.ds(hops * tokens * groups, tokens * groups)
        fkv[0, own, :] = key_ref[...].astype(F32)
        fkv[1, own, :] = value_ref[...].astype(F32)
        values[:, d:] = jnp.ones((span, d), BF16)
        for o in range(1, shards):
            rows = pl.ds((hops - o) * tokens * groups, tokens * groups)
            for side in range(2):
                halo_copy(o, side).wait_recv()
                fkv[side, rows, :] = halo[o - 1, side].astype(F32)
        lax.fori_loop(0, groups, one_group, 0)

    anchor = ctx * tokens
    row = lax.broadcasted_iota(jnp.int32, (ROWS, ROWS), 0)
    col = lax.broadcasted_iota(jnp.int32, (ROWS, ROWS), 1)
    lane = lax.broadcasted_iota(jnp.int32, (1, width), 1)
    low = jnp.where(col > row, 0.0, -jnp.inf)
    high = jnp.where(col <= row, 0.0, -jnp.inf)
    factor = math.log2(math.e) / math.sqrt(d)
    offsets = list(range(1, team)) + [0]

    def attn_copy(g, o, owner):
        to = lax.rem(head + o, team)
        place = attn_ref.at[:, pl.ds(pl.multiple_of((owner * groups + g) * ratio * d, ratio * d), ratio * d)]
        if o == 0:
            return pltpu.make_async_copy(attn_stage.at[g, o], place, own_sem.at[g])
        return remote(attn_stage.at[g, o], place, attn_send.at[g, o - 1], attn_recv.at[g, o - 1], {"head": to})

    def one_group(g, _):
        keys[...] = fkv[0, pl.ds(g, span, stride=groups), :].astype(BF16)
        values[:, :d] = fkv[1, pl.ds(g, span, stride=groups), :].astype(BF16)
        for o in offsets:
            b = lax.rem(head + o, team)
            start = pl.multiple_of(reach - WINDOW + b * ROWS, ROWS)
            key_part = keys[pl.ds(start, width), :]
            value_part = values[pl.ds(start, width), :]
            exists = jnp.where(lane + (anchor - reach + start) >= 0, 0.0, -jnp.inf)
            for r in range(ratio):
                q = fq[pl.ds(b * ROWS * heads + g * ratio + r, ROWS, stride=heads), :].astype(BF16)
                attn_stage[g, o, :, r * d : (r + 1) * d] = attend_rows(
                    q, key_part, value_part, exists, low, high, factor
                )
            attn_copy(g, o, head).start()
        return 0

    def step(p, _):
        @pl.when(p == 1)
        def _():
            attention()

        return delta_pair(p, _)

    lax.fori_loop(0, heads // PAIR, step, 0)

    for o in range(1, n):
        go(o, ctx).start()
    mine[ctx] = pair_ref[ctx]
    for o in range(1, n):
        go(o, lax.rem(ctx - o + n, n)).wait_recv()
    state = jnp.zeros((d, d), F32)
    for i in range(n):
        states[i] = state.astype(BF16)
        if i < n - 1:
            sh, sl = split(state)
            move = mine[i, :, :d]
            both = dot(jnp.concatenate((move, move), axis=1), jnp.concatenate((sh, sl), axis=0))
            state = both + mine[i, :, d:].astype(F32)
    for o in range(1, n):
        back(o, ctx).start()
    incoming[ctx] = states[ctx]
    for o in range(1, n):
        back(o, lax.rem(ctx - o + n, n)).wait_recv()

    def delta_copy(o, owner):
        to = lax.rem(head + o, team)
        place = delta_ref.at[:, pl.ds(pl.multiple_of(owner * heads * d, heads * d), heads * d)]
        if o == 0:
            return pltpu.make_async_copy(delta_stage.at[o], place, own_sem.at[groups])
        return remote(delta_stage.at[o], place, delta_send.at[o - 1], delta_recv.at[o - 1], {"head": to})

    for o in offsets:
        rows = pl.ds(pl.multiple_of(lax.rem(head + o, team) * ROWS, ROWS), ROWS)
        for h in range(heads):
            mh, ml = split(moved[h, rows, :])
            sh = incoming[h]
            both = dot(jnp.concatenate((mh, ml), axis=1), jnp.concatenate((sh, sh), axis=0))
            delta_stage[o, :, h * d : (h + 1) * d] = (both + local_part[h, rows, :]).astype(BF16)
        delta_copy(o, head).start()

    for g in range(groups):
        attn_copy(g, 0, head).wait()
        for o in range(1, team):
            attn_copy(g, o, head).wait_send()
            attn_copy(g, o, lax.rem(head - o + team, team)).wait_recv()
    delta_copy(0, head).wait()
    for o in range(1, team):
        delta_copy(o, head).wait_send()
        delta_copy(o, lax.rem(head - o + team, team)).wait_recv()
    for o in range(1, shards):
        for side in range(2):
            halo_copy(o, side).wait_send()
    for o in range(1, n):
        go(o, ctx).wait_send()
        back(o, ctx).wait_send()


def fused(q, k, v, delta_query, delta_key, delta_value, log_decay, beta):
    tokens, heads, d = q.shape
    groups = k.shape[1]
    shards = -(-WINDOW // tokens) + 1
    n, team = lax.axis_size("ctx"), lax.axis_size("head")
    flat = [x.reshape(-1, d) for x in (q, k, v, delta_query, delta_key, delta_value)]
    span = shards * tokens
    vmem, anywhere = pl.BlockSpec(memory_space=pltpu.VMEM), pl.BlockSpec(memory_space=pl.ANY)
    result = jax.ShapeDtypeStruct((ROWS, team * heads * d), BF16)
    sems = pltpu.SemaphoreType.DMA
    return pl.pallas_call(
        functools.partial(fused_kernel, n, heads, groups, tokens, shards),
        in_specs=[vmem] * 8,
        out_specs=[anywhere, anywhere],
        out_shape=[result, result],
        scratch_shapes=[
            pltpu.VMEM((shards - 1, 2, tokens * groups, d), BF16),
            pltpu.VMEM((tokens * heads, d), F32),
            pltpu.VMEM((2, span * groups, d), F32),
            pltpu.VMEM((span, d), BF16),
            pltpu.VMEM((span, 2 * d), BF16),
            pltpu.VMEM((heads, tokens, d), F32),
            pltpu.VMEM((heads, tokens, d), F32),
            pltpu.VMEM((heads, d, 2 * d), BF16),
            pltpu.VMEM((n, d, 2 * d), BF16),
            pltpu.VMEM((n, d, d), BF16),
            pltpu.VMEM((heads, d, d), BF16),
            pltpu.VMEM((groups, team, ROWS, heads // groups * d), BF16),
            pltpu.VMEM((team, ROWS, heads * d), BF16),
            pltpu.VMEM((tokens * heads, d), F32),
            pltpu.VMEM((tokens * heads, d), F32),
            pltpu.VMEM((tokens * heads, d), F32),
            sems((shards - 1, 2)),
            sems((shards - 1, 2)),
            sems((groups + 1,)),
            sems((groups, team - 1)),
            sems((groups, team - 1)),
            sems((team - 1,)),
            sems((team - 1,)),
            sems((n - 1,)),
            sems((n - 1,)),
            sems((n - 1,)),
            sems((n - 1,)),
        ],
        compiler_params=pltpu.CompilerParams(
            vmem_limit_bytes=VMEM_BYTES, collective_id=1, has_side_effects=True
        ),
        cost_estimate=pl.CostEstimate(flops=20_000_000_000, bytes_accessed=12_000_000, transcendentals=5_000_000),
        name="attend_and_delta",
    )(*flat, log_decay, beta)


def shifted(block, distance):
    n = lax.axis_size("ctx")
    return lax.ppermute(block, "ctx", [(i, i + distance) for i in range(n - distance)])


def local(
    attn_query, attn_key, attention_value, delta_query, delta_key, delta_value, log_decay, beta_gate
):
    tokens = attn_query.shape[0]
    heads, team = attn_query.shape[1], lax.axis_size("head")
    hops = -(-WINDOW // tokens)
    n = lax.axis_size("ctx")
    if n == heads and tokens == team * ROWS and WINDOW % tokens == 0 and hops < n:
        return tuple(
            fused(
                attn_query, attn_key, attention_value, delta_query, delta_key, delta_value, log_decay, beta_gate
            )
        )
    keys = [shifted(attn_key, s) for s in range(hops, 0, -1)] + [attn_key]
    values = [shifted(attention_value, s) for s in range(hops, 0, -1)] + [attention_value]
    moved, local_part, pairs = delta_local(delta_query, delta_key, delta_value, log_decay, beta_gate)
    states = incoming_states(pairs)
    attn_local = attend(attn_query, keys, values)
    attn_out = lax.all_to_all(attn_local, "head", split_axis=0, concat_axis=1, tiled=True)
    delta = delta_final(moved, local_part, states)
    delta_out = lax.all_to_all(delta, "head", split_axis=0, concat_axis=1, tiled=True)
    return (attn_out, delta_out)


def solution(mesh):
    placed = (P("ctx", "head", None),) * 6 + (P("head", "ctx"),) * 2
    return jax.shard_map(
        local,
        mesh=mesh,
        in_specs=placed,
        out_specs=(P(("ctx", "head"), None), P(("ctx", "head"), None)),
        check_vma=False,
    )
```

```python
import functools
import math

import jax
import jax.numpy as jnp
from jax import lax
from jax.experimental import pallas as pl
from jax.experimental.pallas import tpu as pltpu
from jax.sharding import PartitionSpec as P

WINDOW = 1024
CHUNK = 128
PAIR = 2
norm_epsilon = 1e-06
F32, BF16 = jnp.float32, jnp.bfloat16
VMEM_BYTES = 56 * 1024 * 1024


def dot(a, b):
    return lax.dot_general(a, b, (((1,), (0,)), ((), ())), preferred_element_type=F32)


def dot_nt(a, b):
    return lax.dot_general(a, b, (((1,), (1,)), ((), ())), preferred_element_type=F32)


def split(x):
    high = x.astype(BF16)
    return high, (x - high.astype(F32)).astype(BF16)


def dot_square(a, b):
    ah, al = split(a)
    bh, bl = split(b)
    right = jnp.concatenate((bh, bl), axis=1)
    both = dot(jnp.concatenate((ah, al), axis=1), jnp.concatenate((right, right), axis=0))
    width = b.shape[1]
    return both[:, :width] + both[:, width:]


def dot_wide(a, b):
    ah, al = split(a)
    bh, bl = split(b)
    return dot(jnp.concatenate((ah, al), axis=1), jnp.concatenate((bh, bh), axis=0)) + dot(ah, bl)


def row_cumsum(row, upper):
    a = row.astype(BF16)
    rest = row - a.astype(F32)
    b = rest.astype(BF16)
    c = (rest - b.astype(F32)).astype(BF16)
    return dot(a, upper) + (dot(b, upper) + dot(c, upper))


def delta_spans(parts, head_dim):
    size = CHUNK
    row = lax.broadcasted_iota(jnp.int32, (size, size), 0)
    col = lax.broadcasted_iota(jnp.int32, (size, size), 1)
    upper = (row <= col).astype(BF16)
    eye = (row == col).astype(F32)
    state = []
    for q, k, v, log_row, beta_row in parts:
        qb, kb = q.astype(BF16), k.astype(BF16)
        rk = lax.rsqrt(jnp.sum(k * k, axis=1, keepdims=True) + norm_epsilon)
        rq = lax.rsqrt(jnp.sum(q * q, axis=1, keepdims=True) + norm_epsilon) / math.sqrt(head_dim)
        g = row_cumsum(jnp.broadcast_to(log_row, (8, size)), upper)[0:1, :]
        g_row = jnp.broadcast_to(g, (size, size))
        g_col = g_row.T
        b_col = jnp.broadcast_to(beta_row, (size, size)).T
        rk_row = jnp.broadcast_to(rk, (size, size)).T
        ratio = jnp.exp(jnp.where(row >= col, g_col - g_row, -jnp.inf)) * rk_row
        strict = jnp.where(row > col, b_col * rk * ratio * dot_nt(kb, kb), 0.0)
        causal = rq * ratio * dot_nt(qb, kb)
        state.append((strict, causal, g_col, b_col, rk, rq, g))
    inverse = []
    first = (row // 2 == col // 2) & (row > col)
    for s in state:
        inverse.append(eye - jnp.where(first, s[0], 0.0))
    block = 2
    while block < size:
        mask = (row // (2 * block) == col // (2 * block)) & (row // block > col // block)
        half = [dot_square(t, jnp.where(mask, s[0], 0.0)) for t, s in zip(inverse, state)]
        inverse = [t - dot_square(x, t) for t, x in zip(inverse, half)]
        block *= 2
    out = []
    for (q, k, v, _, _), t, (strict, causal, g_col, b_col, rk, rq, g) in zip(parts, inverse, state):
        lead = jnp.exp(g_col)
        weighted = dot_wide(t, jnp.concatenate((b_col * lead * rk * k, b_col * v), axis=1))
        mixed = dot_wide(causal, weighted)
        queries = lead * rq * q - mixed[:, :head_dim]
        last = g[:, size - 1 : size]
        trail = jnp.exp(last - g_col) * rk
        th, tl = split(jnp.concatenate((trail, trail), axis=1) * weighted)
        kt = k.T.astype(BF16)
        written = dot(jnp.concatenate((kt, kt), axis=1), jnp.concatenate((th, tl), axis=0))
        out.append((queries, mixed[:, head_dim:], jnp.exp(last), written))
    return out


def compose(spans, head_dim):
    zeros = jnp.zeros((head_dim, head_dim), F32)
    r = lax.broadcasted_iota(jnp.int32, (head_dim, head_dim), 0)
    c = lax.broadcasted_iota(jnp.int32, (head_dim, head_dim), 1)
    eye = (r == c).astype(F32)
    carried, results = None, []
    for queries, mixed, keep, written in spans:
        if carried is None:
            results.append((queries, mixed))
            carried = jnp.concatenate((keep * eye - written[:, :head_dim], written[:, head_dim:]), axis=1)
        else:
            both = dot_wide(queries, carried)
            results.append((both[:, :head_dim], both[:, head_dim:] + mixed))
            step = dot_wide(written[:, :head_dim], carried)
            carried = keep * carried - step + jnp.concatenate((zeros, written[:, head_dim:]), axis=1)
    return results, carried


def delta_kernel(heads, tokens, q_ref, k_ref, v_ref, log_ref, beta_ref, moved_ref, local_ref, pair_ref, fq, fk, fv):
    head_dim = q_ref.shape[1]

    @pl.when(pl.program_id(0) == 0)
    def _():
        fq[...] = q_ref[...].astype(F32)
        fk[...] = k_ref[...].astype(F32)
        fv[...] = v_ref[...].astype(F32)

    count = tokens // CHUNK
    parts = []
    for j in range(PAIR):
        h = pl.program_id(0) * PAIR + j
        for c in range(count):
            rows = pl.ds(c * CHUNK * heads + h, CHUNK, stride=heads)
            lanes = slice(c * CHUNK, (c + 1) * CHUNK)
            pick = lax.broadcasted_iota(jnp.int32, (heads, CHUNK), 0) == h
            gates = [
                jnp.sum(jnp.where(pick, ref[:, lanes], 0.0), axis=0, keepdims=True) for ref in (log_ref, beta_ref)
            ]
            parts.append((fq[rows, :], fk[rows, :], fv[rows, :], *gates))
    spans = delta_spans(parts, head_dim)
    for j in range(PAIR):
        results, carried = compose(spans[j * count : (j + 1) * count], head_dim)
        for c, (moved, local_part) in enumerate(results):
            moved_ref[j, c * CHUNK : (c + 1) * CHUNK, :] = moved
            local_ref[j, c * CHUNK : (c + 1) * CHUNK, :] = local_part
        pair_ref[j] = carried.astype(pair_ref.dtype)


def delta_local(q, k, v, log_decay, beta):
    tokens, heads, d = q.shape
    flat = [x.reshape(tokens * heads, d) for x in (q, k, v)]
    full = pl.BlockSpec((tokens * heads, d), lambda i: (0, 0))
    gate = pl.BlockSpec((heads, tokens), lambda i: (0, 0))
    per_head = pl.BlockSpec((PAIR, tokens, d), lambda i: (i, 0, 0))
    return pl.pallas_call(
        functools.partial(delta_kernel, heads, tokens),
        grid=(heads // PAIR,),
        in_specs=[full, full, full, gate, gate],
        out_specs=[per_head, per_head, pl.BlockSpec((PAIR, d, 2 * d), lambda i: (i, 0, 0))],
        out_shape=[
            jax.ShapeDtypeStruct((heads, tokens, d), F32),
            jax.ShapeDtypeStruct((heads, tokens, d), F32),
            jax.ShapeDtypeStruct((heads, d, 2 * d), BF16),
        ],
        scratch_shapes=[pltpu.VMEM((tokens * heads, d), F32)] * 3,
        compiler_params=pltpu.CompilerParams(vmem_limit_bytes=VMEM_BYTES),
        cost_estimate=pl.CostEstimate(flops=10_000_000_000, bytes_accessed=8_000_000, transcendentals=0),
        name="delta_local",
    )(*flat, log_decay, beta)


def prefix_kernel(pair_ref, state_ref):
    n, d = pair_ref.shape[0], pair_ref.shape[1]
    state = jnp.zeros((d, d), F32)
    for i in range(n):
        state_ref[i] = state.astype(state_ref.dtype)
        if i < n - 1:
            sh, sl = split(state)
            move = pair_ref[i, :, :d]
            both = dot(jnp.concatenate((move, move), axis=1), jnp.concatenate((sh, sl), axis=0))
            state = both + pair_ref[i, :, d:].astype(F32)


def final_kernel(moved_ref, local_ref, state_ref, out_ref):
    sh = state_ref[0]
    mh, ml = split(moved_ref[0])
    both = dot(jnp.concatenate((mh, ml), axis=1), jnp.concatenate((sh, sh), axis=0))
    out_ref[...] = (both + local_ref[0]).astype(BF16)


def delta_final(moved, local_part, states):
    heads, tokens, d = moved.shape
    per_head = pl.BlockSpec((1, tokens, d), lambda h: (h, 0, 0))
    return pl.pallas_call(
        final_kernel,
        grid=(heads,),
        in_specs=[per_head, per_head, pl.BlockSpec((1, d, d), lambda h: (h, 0, 0))],
        out_specs=pl.BlockSpec((tokens, d), lambda h: (0, h)),
        out_shape=jax.ShapeDtypeStruct((tokens, heads * d), BF16),
        compiler_params=pltpu.CompilerParams(vmem_limit_bytes=VMEM_BYTES),
        cost_estimate=pl.CostEstimate(flops=2_000_000_000, bytes_accessed=6_000_000, transcendentals=0),
        name="delta_final",
    )(moved, local_part, states)


def incoming_states(pairs):
    heads, d = pairs.shape[0], pairs.shape[1]
    n = lax.axis_size("ctx")
    if n == heads:
        mine = lax.all_to_all(pairs, "ctx", split_axis=0, concat_axis=0, tiled=True)
        states = pl.pallas_call(
            prefix_kernel,
            out_shape=jax.ShapeDtypeStruct((n, d, d), BF16),
            cost_estimate=pl.CostEstimate(flops=500_000_000, bytes_accessed=800_000, transcendentals=0),
            name="prefix",
        )(mine)
        return lax.all_to_all(states, "ctx", split_axis=0, concat_axis=0, tiled=True)
    transit, source = pairs[:, :, :d].astype(F32), pairs[:, :, d:].astype(F32)

    def relay(turn, inbound):
        leaving = jnp.einsum("hij,hjk->hik", transit, inbound, precision=lax.Precision.HIGHEST) + source
        return lax.ppermute(leaving, "ctx", [(i, i + 1) for i in range(n - 1)])

    return lax.fori_loop(0, n - 1, relay, jnp.zeros((heads, d, d), F32)).astype(BF16)


ROWS = 128


def attend_kernel(heads, groups, tokens, q_ref, *refs):
    count = len(refs) - 5
    shards = count // 2
    key_refs, value_refs = refs[:shards], refs[shards:count]
    out_ref, fq, fkv, keys, values = refs[count:]
    d = q_ref.shape[1]
    reach = (shards - 1) * tokens
    ratio = heads // groups
    g = pl.program_id(0)

    @pl.when(g == 0)
    def _():
        fq[...] = q_ref[...].astype(F32)
        for s in range(shards):
            fkv[0, pl.ds(s * tokens * groups, tokens * groups), :] = key_refs[s][...].astype(F32)
            fkv[1, pl.ds(s * tokens * groups, tokens * groups), :] = value_refs[s][...].astype(F32)
        values[:, d:] = jnp.ones((values.shape[0], d), BF16)

    span = reach + tokens
    keys[...] = fkv[0, pl.ds(g, span, stride=groups), :].astype(BF16)
    values[:, :d] = fkv[1, pl.ds(g, span, stride=groups), :].astype(BF16)
    width = WINDOW + ROWS
    anchor = lax.axis_index("ctx") * tokens
    row = lax.broadcasted_iota(jnp.int32, (ROWS, ROWS), 0)
    col = lax.broadcasted_iota(jnp.int32, (ROWS, ROWS), 1)
    lane = lax.broadcasted_iota(jnp.int32, (1, width), 1)
    low = jnp.where(col > row, 0.0, -jnp.inf)
    high = jnp.where(col <= row, 0.0, -jnp.inf)
    factor = math.log2(math.e) / math.sqrt(d)
    for b in range(tokens // ROWS):
        start = reach - WINDOW + b * ROWS
        key_part = keys[start : start + width, :]
        value_part = values[start : start + width, :]
        exists = jnp.where(lane + (anchor - reach + start) >= 0, 0.0, -jnp.inf)
        for r in range(ratio):
            h = g * ratio + r
            q = fq[pl.ds(b * ROWS * heads + h, ROWS, stride=heads), :].astype(BF16)
            scores = dot_nt(q, key_part) + exists
            scores = jnp.concatenate(
                (scores[:, :ROWS] + low, scores[:, ROWS:WINDOW], scores[:, WINDOW:] + high), axis=1
            )
            top = jnp.max(scores, axis=1, keepdims=True)
            weights = jnp.exp2((scores - top) * factor).astype(BF16)
            mixed = dot(weights, value_part)
            out_ref[b * ROWS : (b + 1) * ROWS, r * d : (r + 1) * d] = (mixed[:, :d] / mixed[:, d:]).astype(BF16)


def attend(q, key_shards, value_shards):
    tokens, heads, d = q.shape
    groups = key_shards[0].shape[1]
    shards = len(key_shards)
    flat = [x.reshape(-1, d) for x in (q, *key_shards, *value_shards)]
    span = shards * tokens
    return pl.pallas_call(
        functools.partial(attend_kernel, heads, groups, tokens),
        grid=(groups,),
        in_specs=[pl.BlockSpec(x.shape, lambda g: (0, 0)) for x in flat],
        out_specs=pl.BlockSpec((tokens, heads // groups * d), lambda g: (0, g)),
        out_shape=jax.ShapeDtypeStruct((tokens, heads * d), BF16),
        scratch_shapes=[
            pltpu.VMEM((tokens * heads, d), F32),
            pltpu.VMEM((2, span * groups, d), F32),
            pltpu.VMEM((span, d), BF16),
            pltpu.VMEM((span, 2 * d), BF16),
        ],
        compiler_params=pltpu.CompilerParams(vmem_limit_bytes=VMEM_BYTES),
        cost_estimate=pl.CostEstimate(flops=8_000_000_000, bytes_accessed=4_000_000, transcendentals=5_000_000),
        name="attend",
    )(*flat)


def attend_rows(q, key_part, value_part, exists, low, high, factor):
    d = q.shape[1]
    scores = dot_nt(q, key_part) + exists
    scores = jnp.concatenate((scores[:, :ROWS] + low, scores[:, ROWS:WINDOW], scores[:, WINDOW:] + high), axis=1)
    top = jnp.max(scores, axis=1, keepdims=True)
    weights = jnp.exp2((scores - top) * factor).astype(BF16)
    mixed = dot(weights, value_part)
    return (mixed[:, :d] / mixed[:, d:]).astype(BF16)


def fused_kernel(n, heads, groups, tokens, shards, *refs):
    q_ref, key_ref, value_ref, dq_ref, dk_ref, dv_ref, log_ref, beta_ref, attn_ref, delta_ref = refs[:10]
    halo, fq, fkv, keys, values, moved, local_part, pair_ref, mine, states, incoming, attn_stage, delta_stage = refs[10:23]
    dq, dk, dv = refs[23:26]
    halo_send, halo_recv, own_sem, attn_send, attn_recv, delta_send, delta_recv, go_send, go_recv, back_send, back_recv = refs[26:]
    d = q_ref.shape[1]
    ratio = heads // groups
    reach = (shards - 1) * tokens
    span = reach + tokens
    width = WINDOW + ROWS
    team = tokens // ROWS
    ctx, head = lax.axis_index("ctx"), lax.axis_index("head")

    barrier = pltpu.get_barrier_semaphore()
    for o in range(1, n):
        pl.semaphore_signal(barrier, inc=1, device_id={"ctx": lax.rem(ctx + o, n)}, device_id_type=pl.DeviceIdType.MESH)
    for o in range(1, team):
        pl.semaphore_signal(barrier, inc=1, device_id={"head": lax.rem(head + o, team)}, device_id_type=pl.DeviceIdType.MESH)
    pl.semaphore_wait(barrier, n - 1 + team - 1)

    def remote(src, dst, send, recv, where):
        return pltpu.make_async_remote_copy(
            src_ref=src, dst_ref=dst, send_sem=send, recv_sem=recv, device_id=where,
            device_id_type=pl.DeviceIdType.MESH,
        )

    def go(o, slot):
        to = lax.rem(ctx + o, n)
        return remote(pair_ref.at[to], mine.at[slot], go_send.at[o - 1], go_recv.at[o - 1], {"ctx": to})

    def back(o, slot):
        to = lax.rem(ctx + o, n)
        return remote(states.at[to], incoming.at[slot], back_send.at[o - 1], back_recv.at[o - 1], {"ctx": to})

    def halo_copy(o, side):
        source = (key_ref, value_ref)[side]
        return remote(
            source, halo.at[o - 1, side], halo_send.at[o - 1, side], halo_recv.at[o - 1, side],
            {"ctx": lax.rem(ctx + o, n)},
        )

    hops = shards - 1
    for o in range(1, shards):
        for side in range(2):
            halo_copy(o, side).start()
    dq[...] = dq_ref[...].astype(F32)
    dk[...] = dk_ref[...].astype(F32)
    dv[...] = dv_ref[...].astype(F32)

    def delta_pair(p, _):
        count = tokens // CHUNK
        parts = []
        for j in range(PAIR):
            h = p * PAIR + j
            pick = lax.broadcasted_iota(jnp.int32, (heads, CHUNK), 0) == h
            for c in range(count):
                rows = pl.ds(c * CHUNK * heads + h, CHUNK, stride=heads)
                lanes = slice(c * CHUNK, (c + 1) * CHUNK)
                gates = [
                    jnp.sum(jnp.where(pick, ref[:, lanes], 0.0), axis=0, keepdims=True)
                    for ref in (log_ref, beta_ref)
                ]
                parts.append((dq[rows, :], dk[rows, :], dv[rows, :], *gates))
        spans = delta_spans(parts, d)
        for j in range(PAIR):
            h = p * PAIR + j
            results, carried = compose(spans[j * count : (j + 1) * count], d)
            for c, (one, two) in enumerate(results):
                moved[h, c * CHUNK : (c + 1) * CHUNK, :] = one
                local_part[h, c * CHUNK : (c + 1) * CHUNK, :] = two
            pair_ref[h] = carried.astype(BF16)

            @pl.when(h == ctx)
            def _():
                mine[ctx] = pair_ref[ctx]

            @pl.when(h != ctx)
            def _():
                go(lax.rem(h - ctx + n, n), ctx).start()

        return 0

    def attention():
        fq[...] = q_ref[...].astype(F32)
        own = pl.ds(hops * tokens * groups, tokens * groups)
        fkv[0, own, :] = key_ref[...].astype(F32)
        fkv[1, own, :] = value_ref[...].astype(F32)
        values[:, d:] = jnp.ones((span, d), BF16)
        for o in range(1, shards):
            rows = pl.ds((hops - o) * tokens * groups, tokens * groups)
            for side in range(2):
                halo_copy(o, side).wait_recv()
                fkv[side, rows, :] = halo[o - 1, side].astype(F32)
        lax.fori_loop(0, groups, one_group, 0)

    anchor = ctx * tokens
    row = lax.broadcasted_iota(jnp.int32, (ROWS, ROWS), 0)
    col = lax.broadcasted_iota(jnp.int32, (ROWS, ROWS), 1)
    lane = lax.broadcasted_iota(jnp.int32, (1, width), 1)
    low = jnp.where(col > row, 0.0, -jnp.inf)
    high = jnp.where(col <= row, 0.0, -jnp.inf)
    factor = math.log2(math.e) / math.sqrt(d)
    offsets = list(range(1, team)) + [0]

    def attn_copy(g, o, owner):
        to = lax.rem(head + o, team)
        place = attn_ref.at[:, pl.ds(pl.multiple_of((owner * groups + g) * ratio * d, ratio * d), ratio * d)]
        if o == 0:
            return pltpu.make_async_copy(attn_stage.at[g, o], place, own_sem.at[g])
        return remote(attn_stage.at[g, o], place, attn_send.at[g, o - 1], attn_recv.at[g, o - 1], {"head": to})

    def one_group(g, _):
        keys[...] = fkv[0, pl.ds(g, span, stride=groups), :].astype(BF16)
        values[:, :d] = fkv[1, pl.ds(g, span, stride=groups), :].astype(BF16)
        for o in offsets:
            b = lax.rem(head + o, team)
            start = pl.multiple_of(reach - WINDOW + b * ROWS, ROWS)
            key_part = keys[pl.ds(start, width), :]
            value_part = values[pl.ds(start, width), :]
            exists = jnp.where(lane + (anchor - reach + start) >= 0, 0.0, -jnp.inf)
            for r in range(ratio):
                q = fq[pl.ds(b * ROWS * heads + g * ratio + r, ROWS, stride=heads), :].astype(BF16)
                attn_stage[g, o, :, r * d : (r + 1) * d] = attend_rows(
                    q, key_part, value_part, exists, low, high, factor
                )
            attn_copy(g, o, head).start()
        return 0

    def step(p, _):
        @pl.when(p == 1)
        def _():
            attention()

        return delta_pair(lax.rem(lax.div(ctx, PAIR) + 1 + p, heads // PAIR), _)

    lax.fori_loop(0, heads // PAIR, step, 0)

    for o in range(1, n):
        go(o, lax.rem(ctx - o + n, n)).wait_recv()
    state = jnp.zeros((d, d), F32)
    for i in range(n):
        states[i] = state.astype(BF16)
        if i < n - 1:
            sh, sl = split(state)
            move = mine[i, :, :d]
            both = dot(jnp.concatenate((move, move), axis=1), jnp.concatenate((sh, sl), axis=0))
            state = both + mine[i, :, d:].astype(F32)
    for o in range(1, n):
        back(o, ctx).start()
    incoming[ctx] = states[ctx]
    for o in range(1, n):
        back(o, lax.rem(ctx - o + n, n)).wait_recv()

    def delta_copy(o, owner):
        to = lax.rem(head + o, team)
        place = delta_ref.at[:, pl.ds(pl.multiple_of(owner * heads * d, heads * d), heads * d)]
        if o == 0:
            return pltpu.make_async_copy(delta_stage.at[o], place, own_sem.at[groups])
        return remote(delta_stage.at[o], place, delta_send.at[o - 1], delta_recv.at[o - 1], {"head": to})

    for o in offsets:
        rows = pl.ds(pl.multiple_of(lax.rem(head + o, team) * ROWS, ROWS), ROWS)
        for h in range(heads):
            mh, ml = split(moved[h, rows, :])
            sh = incoming[h]
            both = dot(jnp.concatenate((mh, ml), axis=1), jnp.concatenate((sh, sh), axis=0))
            delta_stage[o, :, h * d : (h + 1) * d] = (both + local_part[h, rows, :]).astype(BF16)
        delta_copy(o, head).start()

    for g in range(groups):
        attn_copy(g, 0, head).wait()
        for o in range(1, team):
            attn_copy(g, o, head).wait_send()
            attn_copy(g, o, lax.rem(head - o + team, team)).wait_recv()
    delta_copy(0, head).wait()
    for o in range(1, team):
        delta_copy(o, head).wait_send()
        delta_copy(o, lax.rem(head - o + team, team)).wait_recv()
    for o in range(1, shards):
        for side in range(2):
            halo_copy(o, side).wait_send()
    for o in range(1, n):
        go(o, ctx).wait_send()
        back(o, ctx).wait_send()


def fused(q, k, v, delta_query, delta_key, delta_value, log_decay, beta):
    tokens, heads, d = q.shape
    groups = k.shape[1]
    shards = -(-WINDOW // tokens) + 1
    n, team = lax.axis_size("ctx"), lax.axis_size("head")
    flat = [x.reshape(-1, d) for x in (q, k, v, delta_query, delta_key, delta_value)]
    span = shards * tokens
    vmem, anywhere = pl.BlockSpec(memory_space=pltpu.VMEM), pl.BlockSpec(memory_space=pl.ANY)
    result = jax.ShapeDtypeStruct((ROWS, team * heads * d), BF16)
    sems = pltpu.SemaphoreType.DMA
    return pl.pallas_call(
        functools.partial(fused_kernel, n, heads, groups, tokens, shards),
        in_specs=[vmem] * 8,
        out_specs=[anywhere, anywhere],
        out_shape=[result, result],
        scratch_shapes=[
            pltpu.VMEM((shards - 1, 2, tokens * groups, d), BF16),
            pltpu.VMEM((tokens * heads, d), F32),
            pltpu.VMEM((2, span * groups, d), F32),
            pltpu.VMEM((span, d), BF16),
            pltpu.VMEM((span, 2 * d), BF16),
            pltpu.VMEM((heads, tokens, d), F32),
            pltpu.VMEM((heads, tokens, d), F32),
            pltpu.VMEM((heads, d, 2 * d), BF16),
            pltpu.VMEM((n, d, 2 * d), BF16),
            pltpu.VMEM((n, d, d), BF16),
            pltpu.VMEM((heads, d, d), BF16),
            pltpu.VMEM((groups, team, ROWS, heads // groups * d), BF16),
            pltpu.VMEM((team, ROWS, heads * d), BF16),
            pltpu.VMEM((tokens * heads, d), F32),
            pltpu.VMEM((tokens * heads, d), F32),
            pltpu.VMEM((tokens * heads, d), F32),
            sems((shards - 1, 2)),
            sems((shards - 1, 2)),
            sems((groups + 1,)),
            sems((groups, team - 1)),
            sems((groups, team - 1)),
            sems((team - 1,)),
            sems((team - 1,)),
            sems((n - 1,)),
            sems((n - 1,)),
            sems((n - 1,)),
            sems((n - 1,)),
        ],
        compiler_params=pltpu.CompilerParams(
            vmem_limit_bytes=VMEM_BYTES, collective_id=1, has_side_effects=True
        ),
        cost_estimate=pl.CostEstimate(flops=20_000_000_000, bytes_accessed=12_000_000, transcendentals=5_000_000),
        name="attend_and_delta",
    )(*flat, log_decay, beta)


def shifted(block, distance):
    n = lax.axis_size("ctx")
    return lax.ppermute(block, "ctx", [(i, i + distance) for i in range(n - distance)])


def local(
    attn_query, attn_key, attention_value, delta_query, delta_key, delta_value, log_decay, beta_gate
):
    tokens = attn_query.shape[0]
    heads, team = attn_query.shape[1], lax.axis_size("head")
    hops = -(-WINDOW // tokens)
    n = lax.axis_size("ctx")
    if n == heads and tokens == team * ROWS and WINDOW % tokens == 0 and hops < n:
        return tuple(
            fused(
                attn_query, attn_key, attention_value, delta_query, delta_key, delta_value, log_decay, beta_gate
            )
        )
    keys = [shifted(attn_key, s) for s in range(hops, 0, -1)] + [attn_key]
    values = [shifted(attention_value, s) for s in range(hops, 0, -1)] + [attention_value]
    moved, local_part, pairs = delta_local(delta_query, delta_key, delta_value, log_decay, beta_gate)
    states = incoming_states(pairs)
    attn_local = attend(attn_query, keys, values)
    attn_out = lax.all_to_all(attn_local, "head", split_axis=0, concat_axis=1, tiled=True)
    delta = delta_final(moved, local_part, states)
    delta_out = lax.all_to_all(delta, "head", split_axis=0, concat_axis=1, tiled=True)
    return (attn_out, delta_out)


def solution(mesh):
    placed = (P("ctx", "head", None),) * 6 + (P("head", "ctx"),) * 2
    return jax.shard_map(
        local,
        mesh=mesh,
        in_specs=placed,
        out_specs=(P(("ctx", "head"), None), P(("ctx", "head"), None)),
        check_vma=False,
    )
```
